256 devices in a mesh: gz: 64 (over x, z, core), gy: 4 (over y).
Axes of the slice: x: 4, y: 4, z: 8, core: 2. Of those that a mesh axis runs over, the one named last changes fastest.
Arguments:
- labels: int32 [256, 512, 512], P('gz', 'gy'), may hold values from 0 to 3
- phase_table: float32 [4], replicated, may hold values from 0.2 to 5
- collector_mask: int32 [2, 256, 512], P(None, 'gz', 'gy'), may hold values 0 or 1
- collector_value: float32 [2], replicated, may hold values from -1 to 1
- source: float32 [256, 512, 512], P('gz', 'gy'), may hold values from -6 to 6
Outputs:
- potential: float32 [256, 512, 512], P('gz', 'gy')
- residual: float32 [256, 512, 512], P('gz', 'gy')
The draws below stay inside these ranges and needn't reach their ends.
All inputs are finite; a program needn't handle non-finite values. No bound on the sum of `collector_mask` on one device may be relied on, other than what follows from the above.
Results may differ from the reference program's by a relative error of at most 0.0003.
Values sent between devices are 32-bit elements; how exact they have to be, the bound alone decides.
No kernel may reach another device: no remote copies, remote signals or barrier semaphores. Data moves between devices by JAX's collectives and lax.ppermute only.
A program may use at most 64 MiB of HBM per device.

```python
import math
import jax
import jax.numpy as jnp
from jax import lax

NX = 512
NY = 512
PHASES = 4
ITERS = 2
NZ = 256


def place_ends(array, stream_key, low, high):
    longest = array.shape.index(max(array.shape))
    spots = []
    for shift in (0, 1):
        where = [jax.random.randint(jax.random.fold_in(stream_key, axis), (), 0, length) for axis, length in enumerate(array.shape)]
        where[longest] = (where[longest] + shift) % array.shape[longest]
        spots.append(tuple(where))
    return array.at[spots[0]].set(low).at[spots[1]].set(high)


def steps_of(key, dims, split, smallest, high):
    level = 1.0
    for dim, shards_of in split:
        steps = jax.random.uniform(jax.random.fold_in(jax.random.fold_in(key, 6), dim), (shards_of,), jnp.float32, smallest / len(split), high / len(split))
        level = level * jnp.repeat(jnp.exp(steps), dims[dim] // shards_of).reshape((-1,) + (1,) * (len(dims) - 1 - dim))
    return level


def normal_values(key, dims, deviation, limit, split=(), held_as=jnp.bfloat16):
    result = jax.random.normal(key, dims, jnp.float32) * deviation
    if len(split) > 0:
        result = steps_of(key, dims, split, -0.22, 0.18) * result
    return jnp.clip(result, min=-limit, max=limit).astype(held_as)


def setup_inputs(seed: int = 0) -> dict:
    key_of = jax.random.split(jax.random.key(seed), 6)
    return {
        "labels": place_ends(jax.random.randint(key_of[0], (NZ, NY, NX), 0, PHASES), jax.random.fold_in(key_of[0], 1), 0, PHASES - 1).astype(jnp.int32),
        "phase_table": jnp.clip(jnp.exp(jax.random.uniform(key_of[1], (PHASES,), jnp.float32, math.log(0.2), math.log(5.0))), 0.2, 5.0),
        "collector_mask": place_ends((jax.random.randint(key_of[2], (2, NZ, NY), 0, 2) < 1).astype(jnp.int32), jax.random.fold_in(key_of[2], 1), 0, 1),
        "collector_value": jnp.clip(jax.random.uniform(key_of[3], (2,), jnp.float32, -1.0, 1.0), -1.0, 1.0),
        "source": normal_values(key_of[4], (NZ, NY, NX), 1.0, 6.0, ((0, 64), (1, 4)), jnp.float32),
    }


HIGHEST = lax.Precision.HIGHEST
line_shift = 0.0016

def harmonic(lower, upper):
    return 2.0 * lower * upper / (lower + upper)

def coefficients(padded):
    face_z = harmonic(padded[:-1, 1:-1, 1:-1], padded[1:, 1:-1, 1:-1])
    face_y = harmonic(padded[1:-1, :-1, 1:-1], padded[1:-1, 1:, 1:-1])
    face_x = harmonic(padded[1:-1, 1:-1, :-1], padded[1:-1, 1:-1, 1:])
    return (face_z, face_y, face_x)

def neighbours(padded, face_z, face_y, face_x):
    beside = face_z[:-1] * padded[:-2, 1:-1, 1:-1] + face_z[1:] * padded[2:, 1:-1, 1:-1]
    beside = beside + face_y[:, :-1] * padded[1:-1, :-2, 1:-1] + face_y[:, 1:] * padded[1:-1, 2:, 1:-1]
    beside = beside + face_x[:, :, :-1] * padded[1:-1, 1:-1, :-2] + face_x[:, :, 1:] * padded[1:-1, 1:-1, 2:]
    return beside

def basis_rows(rows, count):
    cols = jnp.arange(count).astype(rows.dtype)
    angle = jnp.pi * (rows[:, None] + 0.5) * cols[None, :] / count
    weight = jnp.where(cols == 0, math.sqrt(1.0 / count), math.sqrt(2.0 / count))
    return jnp.cos(angle) * weight[None, :]

def inverse_values(count, dtype):
    cols = jnp.arange(count).astype(dtype)
    return 1.0 / (line_shift + 2.0 - 2.0 * jnp.cos(jnp.pi * cols / count))

def lookup(labels, phase_table):
    conductivity = jnp.zeros(labels.shape, phase_table.dtype)
    for phase in range(phase_table.shape[0]):
        conductivity = conductivity + jnp.where(labels == phase, phase_table[phase], 0.0)
    return conductivity

def reference(labels, phase_table, collector_mask, collector_value, source):
    conductivity = lookup(labels, phase_table)
    face_z, face_y, face_x = coefficients(jnp.pad(conductivity, 1))
    column = lax.broadcasted_iota(jnp.int32, conductivity.shape, 2)
    masks = collector_mask.astype(conductivity.dtype)
    low_edge = jnp.where(column == 0, 2.0 * conductivity * masks[0][:, :, None], 0.0)
    high_edge = jnp.where(column == NX - 1, 2.0 * conductivity * masks[1][:, :, None], 0.0)
    diagonal = face_z[:-1] + face_z[1:] + (face_y[:, :-1] + face_y[:, 1:]) + (face_x[:, :, :-1] + face_x[:, :, 1:])
    diagonal = diagonal + low_edge + high_edge
    right_side = source + low_edge * collector_value[0] + high_edge * collector_value[1]
    scale = lax.rsqrt(diagonal)
    basis = basis_rows(jnp.arange(NY).astype(source.dtype), NY)
    inverse = inverse_values(NY, source.dtype)

    def operate(field):
        return diagonal * field - neighbours(jnp.pad(field, 1), face_z, face_y, face_x)

    def precondition(values):
        scaled = values * scale
        spectrum = jnp.einsum('yj,zyx->zjx', basis, scaled, precision=HIGHEST) * inverse[None, :, None]
        return scale * jnp.einsum('yj,zjx->zyx', basis, spectrum, precision=HIGHEST)
    potential = jnp.zeros_like(source)
    residual = right_side
    pre = precondition(residual)
    direction = pre
    product = jnp.sum(residual * pre)
    for iteration in range(ITERS):
        image = operate(direction)
        step_length = product / jnp.sum(direction * image)
        potential = potential + step_length * direction
        residual = residual - step_length * image
        if iteration + 1 < ITERS:
            pre = precondition(residual)
            product_next = jnp.sum(residual * pre)
            direction = pre + product_next / product * direction
            product = product_next
    return (potential, residual)
```

```python
import math

import jax
import jax.numpy as jnp
import ml_dtypes
import numpy as np
from jax import lax
from jax.experimental import pallas as pl
from jax.experimental.pallas import tpu as pltpu
from jax.sharding import PartitionSpec as P

F32 = jnp.float32
SHIFT = 0.0016
VMEM = pl.BlockSpec(memory_space=pltpu.VMEM)
SMEM = pl.BlockSpec(memory_space=pltpu.SMEM)
ALL = ("gz", "gy")


def line_tables(total, parts):
    rows = total // parts
    theta = math.acosh(1.0 + SHIFT / 2.0)
    near = np.cosh(theta * (np.arange(total) + 0.5))
    far = near[::-1]
    norm = math.sinh(theta) * math.sinh(total * theta)
    at = np.arange(total)
    green = np.where(at[:, None] <= at[None, :], near[:, None] * far[None, :], far[:, None] * near[None, :]) / norm
    blocks, vectors, scalars = [], [], np.zeros((parts, 8))
    for d in range(parts):
        own = slice(d * rows, (d + 1) * rows)
        low, high = math.cosh(theta * d * rows), math.cosh(theta * (d + 1) * rows)
        flow, fhigh = math.cosh(theta * (total - d * rows)), math.cosh(theta * (total - (d + 1) * rows))
        g = green[own, own].astype(np.float32)
        head = g.astype(ml_dtypes.bfloat16)
        tail = (g - head.astype(np.float32)).astype(ml_dtypes.bfloat16)
        blocks.append(np.concatenate([head, tail, head], axis=1))
        columns = [near[own] / high, far[own] / flow, low * far[own] / norm, fhigh * near[own] / norm]
        vectors.append(np.stack([np.broadcast_to(c[:, None], (rows, 128)) for c in columns]))
        for k in range(1, parts):
            if d >= k:
                scalars[d, k] = math.cosh(theta * (d - k + 1) * rows) / low
            else:
                scalars[d, 4 + k] = math.cosh(theta * (total - (d - k + parts) * rows)) / fhigh
    return np.stack(blocks), np.stack(vectors).astype(np.float32), scalars.astype(np.float32)


def call(body, outs, ins, scratch=()):
    return pl.pallas_call(
        body,
        out_shape=[jax.ShapeDtypeStruct(s, F32) for s in outs],
        in_specs=ins,
        out_specs=[VMEM] * len(outs),
        scratch_shapes=list(scratch),
        compiler_params=pltpu.CompilerParams(vmem_limit_bytes=24 * 2**20),
    )


def rows_of(c):
    return pl.ds(pl.multiple_of(c * 8, 8), 8)


def sublane(shape):
    return lax.broadcasted_iota(jnp.int32, shape, 0)


def lane(shape):
    return lax.broadcasted_iota(jnp.int32, shape, 1)


def recip(x):
    return 1.0 / x


def lookup(labels, table):
    low = jnp.where(labels == 1, table[1], table[0])
    high = jnp.where(labels == 3, table[3], table[2])
    return jnp.where(labels >= 2, high, low)


def wide(column, width):
    return jnp.concatenate([column] * (width // 128), axis=1)


def ends(value, low, high):
    return jnp.concatenate([value[:, :128] + low, value[:, 128:-128], value[:, -128:] + high], axis=1)


def local(labels, phase_table, collector_mask, collector_value, source):
    nz, ny, nx = labels.shape
    parts = lax.axis_size("gy")
    layers = lax.axis_size("gz")
    chunks = ny // 8
    block = (nz, ny, nx)
    plane = (1, ny, nx)
    edge = (nz, 8, nx)
    green, vectors, scalars = line_tables(ny * parts, parts)
    green, vectors, scalars = jnp.asarray(green), jnp.asarray(vectors), jnp.asarray(scalars)

    def ring(value, axis, size, step):
        return lax.ppermute(value, axis, [(i, (i + step) % size) for i in range(size)])

    table = 0.5 / phase_table
    zlo = ring(labels[-1:], "gz", layers, 1)
    zhi = ring(labels[:1], "gz", layers, -1)
    ylo = ring(labels[:, -1, :], "gy", parts, 1)
    yhi = ring(labels[:, 0, :], "gy", parts, -1)
    masks = collector_mask.astype(F32)[..., None]

    def faces(labels, table, values, masks, source, k_o, fx_o, fy_o, fz_o, d_o, e_o, b_o):
        for z in range(nz):
            def fill(c, _):
                k_o[z, rows_of(c), :] = lookup(labels[z, rows_of(c), :], table)
                return 0
            lax.fori_loop(0, chunks, fill, 0)
        sub = sublane((8, nx))
        for z in range(nz):
            def body(c, carry):
                at = rows_of(c)
                k = k_o[z, at, :]
                after = k_o[z, rows_of(jnp.minimum(c + 1, chunks - 1)), :]
                up = jnp.where(sub == 7, pltpu.roll(after, 7, 0), pltpu.roll(k, 7, 0))
                fy = jnp.where(sub + c * 8 == ny - 1, 0.0, recip(k + up))
                turned = pltpu.roll(fy, 1, 0)
                d = fy + jnp.where(sub == 0, carry, turned)
                fx = jnp.where(lane((8, nx)) == nx - 1, 0.0, recip(k + pltpu.roll(k, nx - 1, 1)))
                d = d + (fx + pltpu.roll(fx, 1, 1))
                if z > 0:
                    d = d + fz_o[z - 1, at, :]
                if z < nz - 1:
                    fz = recip(k + k_o[z + 1, at, :])
                    fz_o[z, at, :] = fz
                    d = d + fz
                side = lane((8, 128))
                low = jnp.where(side == 0, recip(k[:, :128]) * masks[0, z, at, :], 0.0)
                high = jnp.where(side == 127, recip(k[:, -128:]) * masks[1, z, at, :], 0.0)
                e_o[z, at, :] = jnp.concatenate([low, high], axis=1)
                d_o[z, at, :] = ends(d, low, high)
                b_o[z, at, :] = ends(source[z, at, :], low * values[0], high * values[1])
                fx_o[z, at, :] = fx
                fy_o[z, at, :] = fy
                return turned
            lax.fori_loop(0, chunks, body, jnp.zeros((8, nx), F32), unroll=True)

    k, fx, fy, fz, d, e, b = call(
        faces,
        [block, block, block, (nz - 1, ny, nx), block, (nz, ny, 256), block],
        [VMEM, SMEM, SMEM, VMEM, VMEM],
    )(labels, table, collector_value, masks, source)

    def payloads(my, sums, outs):
        for step, out in enumerate(outs, 1):
            for z in range(nz):
                out[z : z + 1, :] = jnp.where(my + step < parts, sums[z][0], sums[z][1])

    def scaled(table, k, ylo, yhi, zlo, zhi, d, b, vectors, s_o, x_o, fye_o, fze_o, one, two, three):
        my, level = lax.axis_index("gy"), lax.axis_index("gz")
        has_low, has_high = (my > 0).astype(F32), (my < parts - 1).astype(F32)
        has_below, has_above = (level > 0).astype(F32), (level < layers - 1).astype(F32)
        sub = sublane((8, nx))
        sums = []
        for z in range(nz):
            first = has_low * recip(lookup(ylo[z : z + 1, :], table) + k[z, 0:1, :])
            last = has_high * recip(lookup(yhi[z : z + 1, :], table) + k[z, ny - 1 : ny, :])
            fye_o[z, 0:1, :] = first
            fye_o[z, 1:2, :] = last

            def body(c, carry):
                at = rows_of(c)
                diagonal = d[z, at, :]
                diagonal = diagonal + jnp.where(sub + c * 8 == 0, first, 0.0)
                diagonal = diagonal + jnp.where(sub + c * 8 == ny - 1, last, 0.0)
                if z == 0:
                    face = has_below * recip(lookup(zlo[0, at, :], table) + k[z, at, :])
                    fze_o[0, at, :] = face
                    diagonal = diagonal + face
                if z == nz - 1:
                    face = has_above * recip(lookup(zhi[0, at, :], table) + k[z, at, :])
                    fze_o[1, at, :] = face
                    diagonal = diagonal + face
                s = lax.rsqrt(diagonal)
                x = s * b[z, at, :]
                s_o[z, at, :] = s
                x_o[z, at, :] = x
                return (
                    carry[0] + x * wide(vectors[my, 0, at, :], nx),
                    carry[1] + x * wide(vectors[my, 1, at, :], nx),
                )
            zero = jnp.zeros((8, nx), F32)
            right, left = lax.fori_loop(0, chunks, body, (zero, zero))
            sums.append((jnp.sum(right, 0, keepdims=True), jnp.sum(left, 0, keepdims=True)))
        payloads(my, sums, (one, two, three))
        for z in range(nz):
            one[nz + z : nz + z + 1, :] = s_o[z, ny - 1 : ny, :]
            three[nz + z : nz + z + 1, :] = s_o[z, 0:1, :]

    s, x, fye, fze, one, two, three = call(
        scaled,
        [block, block, edge, (2, ny, nx), (2 * nz, nx), (nz, nx), (2 * nz, nx)],
        [SMEM] + [VMEM] * 8,
    )(table, k, ylo, yhi, zlo, zhi, d, b, vectors)

    def lines(x, green, out):
        my = lax.axis_index("gy")
        for z in range(nz):
            head = x[z].astype(jnp.bfloat16)
            tail = (x[z] - head.astype(F32)).astype(jnp.bfloat16)
            stack = jnp.concatenate([head, head, tail], axis=0)
            out[z] = jnp.dot(green[my], stack, preferred_element_type=F32)

    def solved(part, s, x, vectors, scalars, one, two, three, below, above, p_o, low_o, high_o, side_o):
        my = lax.axis_index("gy")
        for z in range(nz):
            got = [r[z : z + 1, :] for r in (one, two, three)]
            left = sum(scalars[my, n + 1] * got[n] for n in range(3))
            right = sum(scalars[my, 5 + n] * got[n] for n in range(3))

            def value(at):
                return part[z, at, :] + (
                    wide(vectors[my, 2, at, :], nx) * left + wide(vectors[my, 3, at, :], nx) * right
                )

            def body(c, _):
                at = rows_of(c)
                p = s[z, at, :] * value(at)
                p_o[z, at, :] = p
                if z == 0:
                    low_o[0, at, :] = p
                if z == nz - 1:
                    high_o[0, at, :] = p
                return 0
            lax.fori_loop(0, chunks, body, 0)
            g = value(pl.ds(0, 8))
            side_o[z, 0:1, :] = below[nz + z : nz + z + 1, :] * ((2.0 + SHIFT) * g[0:1] - g[1:2] - x[z, 0:1, :])
            g = value(pl.ds(ny - 8, 8))
            side_o[z, 1:2, :] = above[nz + z : nz + z + 1, :] * (
                (2.0 + SHIFT) * g[7:8] - g[6:7] - x[z, ny - 1 : ny, :]
            )

    def precondition(x, one, two, three, below, above):
        one, two, three = (ring(v, "gy", parts, n) for n, v in ((1, one), (2, two), (3, three)))
        part = call(lines, [block], [VMEM, VMEM])(x, green)[0]
        if below is None:
            below, above = one, three
        out = call(solved, [block, plane, plane, edge], [VMEM] * 4 + [SMEM] + [VMEM] * 5)(
            part, s, x, vectors, scalars, one, two, three, below, above
        )
        return out, below, above

    def total(value):
        return jnp.sum(jnp.sum(value, 0, keepdims=True), 1, keepdims=True)

    def operator(p, side, fx, fy, fz, fye, e, q_o, z):
        sub = sublane((8, nx))
        bottom = fye[z, 0:1, :] * (side[z, 0:1, :] - p[z, 0:1, :])
        top = fye[z, 1:2, :] * (p[z, ny - 1 : ny, :] - side[z, 1:2, :])

        def body(c, carry):
            at = rows_of(c)
            v = p[z, at, :]
            after = p[z, rows_of(jnp.minimum(c + 1, chunks - 1)), :]
            up = jnp.where(sub == 7, pltpu.roll(after, 7, 0), pltpu.roll(v, 7, 0))
            flow = fy[z, at, :] * (v - up)
            turned = pltpu.roll(flow, 1, 0)
            q = flow - jnp.where(sub == 0, carry, turned)
            q = q + jnp.where(sub + c * 8 == ny - 1, top, 0.0)
            flow = fx[z, at, :] * (v - pltpu.roll(v, nx - 1, 1))
            q = q + (flow - pltpu.roll(flow, 1, 1))
            if z > 0:
                q = q + fz[z - 1, at, :] * (v - p[z - 1, at, :])
            if z < nz - 1:
                q = q + fz[z, at, :] * (v - p[z + 1, at, :])
            edges = e[z, at, :]
            q_o[z, at, :] = ends(q, edges[:, :128] * v[:, :128], edges[:, 128:] * v[:, -128:])
            return turned
        lax.fori_loop(0, chunks, body, jnp.broadcast_to(bottom, (8, nx)), unroll=True)

    def inner(p, side, fx, fy, fz, fye, e, q_o):
        for z in range(nz):
            operator(p, side, fx, fy, fz, fye, e, q_o, z)

    def dots_out(out, sums):
        at = lane((1, 128))
        row = jnp.zeros((1, 128), F32)
        for n, value in enumerate(sums):
            row = jnp.where(at == n, total(value), row)
        out[0:1, :] = row

    def outer_first(p, q, zlo, zhi, fze, s, b, vectors, q_o, x_o, one, two, three, dots):
        my = lax.axis_index("gy")
        zero = jnp.zeros((8, nx), F32)
        bp, pq = zero, zero
        sums = []
        for z in range(nz):
            def body(c, carry):
                at = rows_of(c)
                v, image = p[z, at, :], q[z, at, :]
                if z == 0:
                    image = image + fze[0, at, :] * (v - zlo[0, at, :])
                if z == nz - 1:
                    image = image + fze[1, at, :] * (v - zhi[0, at, :])
                x = s[z, at, :] * image
                q_o[z, at, :] = image
                x_o[z, at, :] = x
                return (
                    carry[0] + x * wide(vectors[my, 0, at, :], nx),
                    carry[1] + x * wide(vectors[my, 1, at, :], nx),
                    carry[2] + b[z, at, :] * v,
                    carry[3] + v * image,
                )
            right, left, bp, pq = lax.fori_loop(0, chunks, body, (zero, zero, bp, pq))
            sums.append((jnp.sum(right, 0, keepdims=True), jnp.sum(left, 0, keepdims=True)))
        payloads(my, sums, (one, two, three))
        dots_out(dots, (bp, pq))

    def outer_last(w, v, zlo, zhi, fze, b, q, first, v_o, dots):
        zero = jnp.zeros((8, nx), F32)
        carry = (zero, zero, zero)
        for z in range(nz):
            def body(c, carry):
                at = rows_of(c)
                field, image = w[z, at, :], v[z, at, :]
                if z == 0:
                    image = image + fze[0, at, :] * (field - zlo[0, at, :])
                if z == nz - 1:
                    image = image + fze[1, at, :] * (field - zhi[0, at, :])
                v_o[z, at, :] = image
                return (
                    carry[0] + b[z, at, :] * field,
                    carry[1] + q[z, at, :] * field,
                    carry[2] + image * field,
                )
            carry = lax.fori_loop(0, chunks, body, carry)
        at = lane((1, 128))
        row = first[...]
        for n, value in enumerate(carry):
            row = jnp.where(at == n + 2, total(value), row)
        dots[...] = row

    def combine(gathered, p, w, q, v, b, x_o, r_o):
        sums = jnp.sum(gathered[...], 0, keepdims=True)
        at = lane((1, 128))
        bp, pq, bw, qw, wv = (jnp.sum(jnp.where(at == n, sums, 0.0), 1, keepdims=True) for n in range(5))
        step = bp / pq
        product = bp - step * (bw + pq) + step * step * qw
        more = 1.0 + product / bp
        curvature = more * more * pq - 2.0 * more * step * qw + step * step * wv
        second = product / curvature
        along, across = step + second * more, second * step
        for z in range(nz):
            def body(c, _):
                at = rows_of(c)
                x_o[z, at, :] = along * p[z, at, :] - across * w[z, at, :]
                r_o[z, at, :] = b[z, at, :] - along * q[z, at, :] + across * v[z, at, :]
                return 0
            lax.fori_loop(0, chunks, body, 0)

    def image_part(p, side):
        return call(inner, [block], [VMEM] * 7)(p, side, fx, fy, fz, fye, e)[0]

    (p, low, high, side), below, above = precondition(x, one, two, three, None, None)
    zlo, zhi = ring(high, "gz", layers, 1), ring(low, "gz", layers, -1)
    q, x, one, two, three, dots = call(
        outer_first, [block, block, (nz, nx), (nz, nx), (nz, nx), (1, 128)], [VMEM] * 8
    )(p, image_part(p, side), zlo, zhi, fze, s, b, vectors)
    (w, low, high, side), _, _ = precondition(x, one, two, three, below, above)
    zlo, zhi = ring(high, "gz", layers, 1), ring(low, "gz", layers, -1)
    v, dots = call(outer_last, [block, (1, 128)], [VMEM] * 8)(w, image_part(w, side), zlo, zhi, fze, b, q, dots)
    count = parts * layers
    gathered = lax.all_to_all(jnp.broadcast_to(dots, (count, 128)), ALL, 0, 0, tiled=True)
    return tuple(call(combine, [block, block], [VMEM] * 6)(gathered, p, w, q, v, b))


def solution(mesh):
    return jax.shard_map(
        local,
        mesh=mesh,
        in_specs=(P("gz", "gy", None), P(), P(None, "gz", "gy"), P(), P("gz", "gy", None)),
        out_specs=(P("gz", "gy", None), P("gz", "gy", None)),
        check_vma=False,
    )
```

```python
import math

import jax
import jax.numpy as jnp
import ml_dtypes
import numpy as np
from jax import lax
from jax.experimental import pallas as pl
from jax.experimental.pallas import tpu as pltpu
from jax.sharding import PartitionSpec as P

F32 = jnp.float32
SHIFT = 0.0016
VMEM = pl.BlockSpec(memory_space=pltpu.VMEM)
HBM = pl.BlockSpec(memory_space=pltpu.HBM)
SMEM = pl.BlockSpec(memory_space=pltpu.SMEM)
ALL = ("gz", "gy")
STEP = 64


def line_tables(total, parts):
    rows = total // parts
    theta = math.acosh(1.0 + SHIFT / 2.0)
    near = np.cosh(theta * (np.arange(total) + 0.5))
    far = near[::-1]
    norm = math.sinh(theta) * math.sinh(total * theta)
    at = np.arange(total)
    green = np.where(at[:, None] <= at[None, :], near[:, None] * far[None, :], far[:, None] * near[None, :]) / norm
    blocks, vectors, scalars = [], [], np.zeros((parts, 8))
    for d in range(parts):
        own = slice(d * rows, (d + 1) * rows)
        low, high = math.cosh(theta * d * rows), math.cosh(theta * (d + 1) * rows)
        flow, fhigh = math.cosh(theta * (total - d * rows)), math.cosh(theta * (total - (d + 1) * rows))
        g = green[own, own].astype(np.float32)
        head = g.astype(ml_dtypes.bfloat16)
        tail = (g - head.astype(np.float32)).astype(ml_dtypes.bfloat16)
        blocks.append(np.concatenate([head, tail, head], axis=1))
        columns = [near[own] / high, far[own] / flow, low * far[own] / norm, fhigh * near[own] / norm]
        vectors.append(np.stack([np.broadcast_to(c[:, None], (rows, 128)) for c in columns]))
        for k in range(1, parts):
            if d >= k:
                scalars[d, k] = math.cosh(theta * (d - k + 1) * rows) / low
            else:
                scalars[d, 4 + k] = math.cosh(theta * (total - (d - k + parts) * rows)) / fhigh
    return np.stack(blocks), np.stack(vectors).astype(np.float32), scalars.astype(np.float32)


def call(body, outs, ins, scratch=(), dtype=F32, out_space=VMEM):
    return pl.pallas_call(
        body,
        out_shape=[jax.ShapeDtypeStruct(s, dtype) for s in outs],
        in_specs=ins,
        out_specs=[out_space] * len(outs),
        scratch_shapes=list(scratch),
        compiler_params=pltpu.CompilerParams(vmem_limit_bytes=24 * 2**20),
    )


def rows_at(start):
    return slice(start, start + STEP)


def sublane(shape):
    return lax.broadcasted_iota(jnp.int32, shape, 0)


def lane(shape):
    return lax.broadcasted_iota(jnp.int32, shape, 1)


def recip(x):
    r = pl.reciprocal(x, approx=True)
    return r * (2.0 - x * r)


def fold(x):
    return sum(x[r : r + 8] for r in range(0, x.shape[0], 8))


def folded(x):
    x = fold(x)
    return sum(x[:, c : c + 128] for c in range(0, x.shape[1], 128))


def lookup(labels, table):
    low = jnp.where(labels == 1, table[1], table[0])
    high = jnp.where(labels == 3, table[3], table[2])
    return jnp.where(labels >= 2, high, low)


def wide(column, width):
    return jnp.concatenate([column] * (width // 128), axis=1)


def ends(value, low, high):
    return jnp.concatenate([value[:, :128] + low, value[:, 128:-128], value[:, -128:] + high], axis=1)


def local(labels, phase_table, collector_mask, collector_value, source):
    nz, ny, nx = labels.shape
    parts = lax.axis_size("gy")
    layers = lax.axis_size("gz")
    block = (nz, ny, nx)
    plane = (1, ny, nx)
    edge = (nz, 8, nx)
    framed = (nz, ny + 16, nx)
    starts = range(0, ny, STEP)
    outer = sorted({0, nz - 1})
    middle = [z for z in range(nz) if z not in outer]
    ends_shape, middle_shape = (len(outer), ny, nx), (len(middle), ny, nx)
    green, vectors, scalars = line_tables(ny * parts, parts)
    green, vectors, scalars = jnp.asarray(green), jnp.asarray(vectors), jnp.asarray(scalars)

    def pick(z, first, second):
        return first.at[outer.index(z)] if z in outer else second.at[middle.index(z)]

    def ring(value, axis, size, step):
        return lax.ppermute(value, axis, [(i, (i + step) % size) for i in range(size)])

    def borders(labels, below_o, above_o, first_o, last_o, first, last, sems):
        copies = [
            pltpu.make_async_copy(labels.at[pl.ds(0, 1)], below_o, sems.at[0]),
            pltpu.make_async_copy(labels.at[pl.ds(nz - 1, 1)], above_o, sems.at[1]),
            pltpu.make_async_copy(labels.at[:, pl.ds(0, 8)], first, sems.at[2]),
            pltpu.make_async_copy(labels.at[:, pl.ds(ny - 8, 8)], last, sems.at[3]),
        ]
        for copy in copies:
            copy.start()
        for copy in copies:
            copy.wait()
        for z in range(nz):
            first_o[z : z + 1, :] = first[z, 0:1, :]
            last_o[z : z + 1, :] = last[z, 7:8, :]

    below, above, first, last = call(
        borders,
        [plane, plane, (nz, nx), (nz, nx)],
        [HBM],
        [pltpu.VMEM(edge, jnp.int32)] * 2 + [pltpu.SemaphoreType.DMA((4,))],
        jnp.int32,
    )(labels)
    table = 0.5 / phase_table
    ylo, yhi = ring(last, "gy", parts, 1), ring(first, "gy", parts, -1)
    zlo, zhi = ring(above, "gz", layers, 1), ring(below, "gz", layers, -1)
    masks = collector_mask.astype(F32)[..., None]

    def faces(labels, table, values, masks, source, k_o, fx_o, fy_o, fz_o, d_o, e_o, b_o, held, framed_k, sem):
        copy = pltpu.make_async_copy(source, held, sem)
        copy.start()
        for z in range(nz):
            for r in starts:
                k = lookup(labels[z, rows_at(r), :], table)
                k_o[z, rows_at(r), :] = k
                framed_k[z, rows_at(r + 8), :] = k
            framed_k[z, ny + 8 : ny + 16, :] = framed_k[z, ny : ny + 8, :]
            fy_o[z, 0:8, :] = jnp.zeros((8, nx), F32)
        copy.wait()
        sub, across, side = sublane((STEP, nx)), lane((STEP, nx)), lane((STEP, 128))
        for z in range(nz):
            for r in starts:
                at = rows_at(r)
                k = k_o[z, at, :]
                fy = recip(k + framed_k[z, rows_at(r + 9), :])
                if r + STEP == ny:
                    fy = jnp.where(sub == STEP - 1, 0.0, fy)
                fy_o[z, rows_at(r + 8), :] = fy
                fx = jnp.where(across == nx - 1, 0.0, recip(k + pltpu.roll(k, nx - 1, 1)))
                d = fy + fy_o[z, rows_at(r + 7), :] + (fx + pltpu.roll(fx, 1, 1))
                if z > 0:
                    d = d + fz_o[z - 1, at, :]
                if z < nz - 1:
                    fz = recip(k + k_o[z + 1, at, :])
                    fz_o[z, at, :] = fz
                    d = d + fz
                low = jnp.where(side == 0, recip(k[:, :128]) * masks[0, z, at, :], 0.0)
                high = jnp.where(side == 127, recip(k[:, -128:]) * masks[1, z, at, :], 0.0)
                e_o[z, at, :] = jnp.concatenate([low, high], axis=1)
                d_o[z, at, :] = ends(d, low, high)
                b_o[z, at, :] = ends(held[z, at, :], low * values[0], high * values[1])
                fx_o[z, at, :] = fx

    k, fx, fy, fz, d, e, b = call(
        faces,
        [block, block, (nz, ny + 8, nx), (nz - 1, ny, nx), block, (nz, ny, 256), block],
        [VMEM, SMEM, SMEM, VMEM, HBM],
        [pltpu.VMEM(block, F32), pltpu.VMEM(framed, F32), pltpu.SemaphoreType.DMA],
    )(labels, table, collector_value, masks, source)

    def weighted(x, my, vectors, r, carry):
        return (
            carry[0] + fold(x * wide(vectors[my, 0, rows_at(r), :], nx)),
            carry[1] + fold(x * wide(vectors[my, 1, rows_at(r), :], nx)),
        )

    def sums_out(my, sums, z, outs):
        right, left = (jnp.sum(v, 0, keepdims=True) for v in sums)
        for step, out in enumerate(outs, 1):
            out[z : z + 1, :] = jnp.where(my + step < parts, right, left)

    zero = lambda: jnp.zeros((8, nx), F32)
    none = lambda: jnp.zeros((8, 128), F32)

    def scaled(table, k, ylo, yhi, zlo, zhi, d, b, vectors, s_o, xo_o, xm_o, fye_o, fze_o, one, two, three):
        my, level = lax.axis_index("gy"), lax.axis_index("gz")
        has_low, has_high = (my > 0).astype(F32), (my < parts - 1).astype(F32)
        has_below, has_above = (level > 0).astype(F32), (level < layers - 1).astype(F32)
        sub = sublane((STEP, nx))
        for z in range(nz):
            first = has_low * recip(lookup(ylo[z : z + 1, :], table) + k[z, 0:1, :])
            last = has_high * recip(lookup(yhi[z : z + 1, :], table) + k[z, ny - 1 : ny, :])
            fye_o[z, 0:1, :] = first
            fye_o[z, 1:2, :] = last
            carry = (zero(), zero())
            for r in starts:
                at = rows_at(r)
                diagonal = d[z, at, :]
                if r == 0:
                    diagonal = diagonal + jnp.where(sub == 0, first, 0.0)
                if r + STEP == ny:
                    diagonal = diagonal + jnp.where(sub == STEP - 1, last, 0.0)
                if z == 0:
                    face = has_below * recip(lookup(zlo[0, at, :], table) + k[z, at, :])
                    fze_o[0, at, :] = face
                    diagonal = diagonal + face
                if z == nz - 1:
                    face = has_above * recip(lookup(zhi[0, at, :], table) + k[z, at, :])
                    fze_o[1, at, :] = face
                    diagonal = diagonal + face
                s = lax.rsqrt(diagonal)
                x = s * b[z, at, :]
                s_o[z, at, :] = s
                pick(z, xo_o, xm_o)[at, :] = x
                carry = weighted(x, my, vectors, r, carry)
            sums_out(my, carry, z, (one, two, three))
            one[nz + z : nz + z + 1, :] = s_o[z, ny - 1 : ny, :]
            three[nz + z : nz + z + 1, :] = s_o[z, 0:1, :]

    s, xo, xm, fye, fze, one, two, three = call(
        scaled,
        [block, ends_shape, middle_shape, edge, (2, ny, nx), (2 * nz, nx), (nz, nx), (2 * nz, nx)],
        [SMEM] + [VMEM] * 8,
    )(table, k, ylo, yhi, zlo, zhi, d, b, vectors)

    def lines(xo, xm, green, out):
        my = lax.axis_index("gy")
        for z in range(nz):
            x = pick(z, xo, xm)[...]
            head = x.astype(jnp.bfloat16)
            tail = (x - head.astype(F32)).astype(jnp.bfloat16)
            stack = jnp.concatenate([head, head, tail], axis=0)
            out[z] = jnp.dot(green[my], stack, preferred_element_type=F32)

    def solve(z, part, s, xo, xm, vectors, scalars, one, two, three, below, above, put):
        my = lax.axis_index("gy")
        got = [r[z : z + 1, :] for r in (one, two, three)]
        left = sum(scalars[my, n + 1] * got[n] for n in range(3))
        right = sum(scalars[my, 5 + n] * got[n] for n in range(3))
        for r in starts:
            at = rows_at(r)
            g = part[z, at, :] + (wide(vectors[my, 2, at, :], nx) * left + wide(vectors[my, 3, at, :], nx) * right)
            put(r + 8, s[z, at, :] * g)
            if r == 0:
                beside = (2.0 + SHIFT) * g[0:1] - g[1:2] - pick(z, xo, xm)[0:1, :]
                put(7, below[nz + z : nz + z + 1, :] * beside)
            if r + STEP == ny:
                beside = (2.0 + SHIFT) * g[-1:] - g[-2:-1] - pick(z, xo, xm)[ny - 1 : ny, :]
                put(ny + 8, above[nz + z : nz + z + 1, :] * beside)

    def solve_outer(part, s, xo, xm, vectors, scalars, one, two, three, below, above, p_o, low_o, high_o):
        for n, z in enumerate(outer):
            def put(r, value):
                p_o[n, r : r + value.shape[0], :] = value
                if z == 0 and value.shape[0] == STEP:
                    low_o[0, rows_at(r - 8), :] = value
                if z == nz - 1 and value.shape[0] == STEP:
                    high_o[0, rows_at(r - 8), :] = value
            solve(z, part, s, xo, xm, vectors, scalars, one, two, three, below, above, put)

    def total(value):
        return jnp.sum(jnp.sum(value, 0, keepdims=True), 1, keepdims=True)

    def dots_out(out, sums, first):
        at = lane((1, 128))
        row = jnp.zeros((1, 128), F32)
        for n, value in enumerate(sums, first):
            row = jnp.where(at == n, total(value), row)
        out[...] = row

    def operator(read, z, r, fx, fy, fz, fye, e):
        at = rows_at(r)
        v = read(z, r + 8)
        q = fy[z, rows_at(r + 8), :] * (v - read(z, r + 9)) + fy[z, rows_at(r + 7), :] * (v - read(z, r + 7))
        sub = sublane((STEP, nx))
        if r == 0:
            q = q + jnp.where(sub == 0, fye[z, 0:1, :], 0.0) * (v - read(z, r + 7))
        if r + STEP == ny:
            q = q + jnp.where(sub == STEP - 1, fye[z, 1:2, :], 0.0) * (v - read(z, r + 9))
        flow = fx[z, at, :] * (v - pltpu.roll(v, nx - 1, 1))
        q = q + (flow - pltpu.roll(flow, 1, 1))
        if z > 0:
            q = q + fz[z - 1, at, :] * (v - read(z - 1, r + 8))
        if z < nz - 1:
            q = q + fz[z, at, :] * (v - read(z + 1, r + 8))
        edges = e[z, at, :]
        return v, ends(q, edges[:, :128] * v[:, :128], edges[:, 128:] * v[:, -128:])

    def fill(part, s, xo, xm, vectors, scalars, one, two, three, below, above, p_outer, p_o, field):
        for z in middle:
            def put(r, value):
                field[z, r : r + value.shape[0], :] = value
                if value.shape[0] == STEP:
                    p_o[z, rows_at(r - 8), :] = value
            solve(z, part, s, xo, xm, vectors, scalars, one, two, three, below, above, put)
        for n, z in enumerate(outer):
            for r in starts:
                p_o[z, rows_at(r), :] = p_outer[n, rows_at(r + 8), :]

        def read(z, r):
            return p_outer[outer.index(z), rows_at(r), :] if z in outer else field[z, rows_at(r), :]
        return read

    def inner_first(part, s, xo, xm, vectors, scalars, one, two, three, below, above, p_outer, fx, fy, fz, fye, e, b,
                    p_o, q_o, xm_o, one_o, two_o, three_o, dots, field):
        my = lax.axis_index("gy")
        read = fill(part, s, xo, xm, vectors, scalars, one, two, three, below, above, p_outer, p_o, field)
        bp, pq = none(), none()
        for z in outer + middle:
            carry = (zero(), zero())
            for r in starts:
                at = rows_at(r)
                v, image = operator(read, z, r, fx, fy, fz, fye, e)
                bp = bp + folded(b[z, at, :] * v)
                q_o[z, at, :] = image
                if z in middle:
                    scaled_image = s[z, at, :] * image
                    xm_o[middle.index(z), at, :] = scaled_image
                    carry = weighted(scaled_image, my, vectors, r, carry)
                    pq = pq + folded(v * image)
            if z in middle:
                sums_out(my, carry, z, (one_o, two_o, three_o))
        dots_out(dots, (bp, pq), 0)

    def image_of(z, ends, whole, at):
        return ends[outer.index(z), at, :] if z in outer else whole[z, at, :]

    def outside(z, r, v, image, zlo, zhi, fze):
        at = rows_at(r)
        if z == 0:
            image = image + fze[0, at, :] * (v - zlo[0, at, :])
        if z == nz - 1:
            image = image + fze[1, at, :] * (v - zhi[0, at, :])
        return image

    def outer_first(p, q, one, two, three, zlo, zhi, fze, s, vectors, dots, qo_o, xo_o, one_o, two_o, three_o, dots_o):
        my = lax.axis_index("gy")
        pq = none()
        for z in outer:
            carry = (zero(), zero())
            for r in starts:
                at = rows_at(r)
                v = p[z, at, :]
                image = outside(z, r, v, q[z, at, :], zlo, zhi, fze)
                scaled_image = s[z, at, :] * image
                qo_o[outer.index(z), at, :] = image
                xo_o[outer.index(z), at, :] = scaled_image
                carry = weighted(scaled_image, my, vectors, r, carry)
                pq = pq + folded(v * image)
            sums_out(my, carry, z, (one_o, two_o, three_o))
        for z in middle:
            for got, out in ((one, one_o), (two, two_o), (three, three_o)):
                out[z : z + 1, :] = got[z : z + 1, :]
        dots_out(dots_o, (none(), pq), 0)
        dots_o[...] = dots_o[...] + dots[...]

    def inner_last(part, s, xo, xm, vectors, scalars, one, two, three, below, above, p_outer, fx, fy, fz, fye, e, b, q, qo,
                   w_o, v_o, dots, field):
        read = fill(part, s, xo, xm, vectors, scalars, one, two, three, below, above, p_outer, w_o, field)
        bw, qw, wv = none(), none(), none()
        for z in range(nz):
            for r in starts:
                at = rows_at(r)
                w, image = operator(read, z, r, fx, fy, fz, fye, e)
                bw = bw + folded(b[z, at, :] * w)
                qw = qw + folded(image_of(z, qo, q, at) * w)
                wv = wv + folded(image * w)
                v_o[z, at, :] = image
        dots_out(dots, (bw, qw, wv), 2)

    def outer_last(w, v, zlo, zhi, fze, dots_first, dots, v_o, dots_o):
        wv = none()
        for n, z in enumerate(outer):
            for r in starts:
                at = rows_at(r)
                field, image = w[z, at, :], v[z, at, :]
                full = outside(z, r, field, image, zlo, zhi, fze)
                v_o[n, at, :] = full
                wv = wv + folded((full - image) * field)
        dots_out(dots_o, (wv,), 4)
        dots_o[...] = dots_o[...] + (dots[...] + dots_first[...])

    def combine(gathered, p, w, q, qo, v, vo, b, x_o, r_o, x_held, r_held, sems):
        sums = jnp.sum(gathered[...], 0, keepdims=True)
        at = lane((1, 128))
        bp, pq, bw, qw, wv = (jnp.sum(jnp.where(at == n, sums, 0.0), 1, keepdims=True) for n in range(5))
        step = bp / pq
        product = bp - step * (bw + pq) + step * step * qw
        more = 1.0 + product / bp
        curvature = more * more * pq - 2.0 * more * step * qw + step * step * wv
        second = product / curvature
        along = jnp.broadcast_to(step + second * more, (STEP, nx))
        across = jnp.broadcast_to(second * step, (STEP, nx))
        copies = []
        for z in range(nz):
            for r in starts:
                at = rows_at(r)
                x_held[z, at, :] = along * p[z, at, :] - across * w[z, at, :]
                r_held[z, at, :] = b[z, at, :] - along * image_of(z, qo, q, at) + across * image_of(z, vo, v, at)
            for n, (held, out) in enumerate(((x_held, x_o), (r_held, r_o))):
                copies.append(pltpu.make_async_copy(held.at[z], out.at[z], sems.at[n, z]))
                copies[-1].start()
        for copy in copies:
            copy.wait()

    def gather(sums):
        return [ring(v, "gy", parts, n) for n, v in enumerate(sums, 1)]

    field = [pltpu.VMEM(framed, F32)]
    rows = [(nz, nx)] * 3
    framed_pair = (len(outer), ny + 16, nx)

    def start(xo, xm, sums, beside):
        got = gather(sums)
        beside = beside or (got[0], got[2])
        part = call(lines, [block], [VMEM] * 3)(xo, xm, green)[0]
        known = (part, s, xo, xm, vectors, scalars, *got, *beside)
        pair, low, high = call(solve_outer, [framed_pair, plane, plane], places)(*known)
        return (*known, pair), ring(high, "gz", layers, 1), ring(low, "gz", layers, -1), beside

    places = [VMEM] * 5 + [SMEM] + [VMEM] * 5
    known, zlo, zhi, beside = start(xo, xm, (one, two, three), None)
    p, q, xm, *sums, dots = call(
        inner_first, [block, block, middle_shape, *rows, (1, 128)], places + [VMEM] * 7, field
    )(*known, fx, fy, fz, fye, e, b)
    qo, xo, *sums, dots = call(outer_first, [ends_shape, ends_shape, *rows, (1, 128)], [VMEM] * 11)(
        p, q, *sums, zlo, zhi, fze, s, vectors, dots
    )
    known, zlo, zhi, _ = start(xo, xm, sums, beside)
    w, v, last_dots = call(inner_last, [block, block, (1, 128)], places + [VMEM] * 9, field)(
        *known, fx, fy, fz, fye, e, b, q, qo
    )
    vo, dots = call(outer_last, [ends_shape, (1, 128)], [VMEM] * 7)(w, v, zlo, zhi, fze, last_dots, dots)
    count = parts * layers
    gathered = lax.all_to_all(jnp.broadcast_to(dots, (count, 128)), ALL, 0, 0, tiled=True)
    return tuple(
        call(
            combine,
            [block, block],
            [VMEM] * 8,
            [pltpu.VMEM(block, F32)] * 2 + [pltpu.SemaphoreType.DMA((2, nz))],
            out_space=HBM,
        )(gathered, p, w, q, qo, v, vo, b)
    )


def solution(mesh):
    return jax.shard_map(
        local,
        mesh=mesh,
        in_specs=(P("gz", "gy", None), P(), P(None, "gz", "gy"), P(), P("gz", "gy", None)),
        out_specs=(P("gz", "gy", None), P("gz", "gy", None)),
        check_vma=False,
    )
```

```python
import math

import jax
import jax.numpy as jnp
import ml_dtypes
import numpy as np
from jax import lax
from jax.experimental import pallas as pl
from jax.experimental.pallas import tpu as pltpu
from jax.sharding import PartitionSpec as P

F32 = jnp.float32
SHIFT = 0.0016
VMEM = pl.BlockSpec(memory_space=pltpu.VMEM)
HBM = pl.BlockSpec(memory_space=pltpu.HBM)
SMEM = pl.BlockSpec(memory_space=pltpu.SMEM)
ALL = ("gz", "gy")
STEP = 64


def line_tables(total, parts):
    rows = total // parts
    theta = math.acosh(1.0 + SHIFT / 2.0)
    near = np.cosh(theta * (np.arange(total) + 0.5))
    far = near[::-1]
    norm = math.sinh(theta) * math.sinh(total * theta)
    at = np.arange(total)
    green = np.where(at[:, None] <= at[None, :], near[:, None] * far[None, :], far[:, None] * near[None, :]) / norm
    blocks, vectors, scalars = [], [], np.zeros((parts, 8))
    for d in range(parts):
        own = slice(d * rows, (d + 1) * rows)
        low, high = math.cosh(theta * d * rows), math.cosh(theta * (d + 1) * rows)
        flow, fhigh = math.cosh(theta * (total - d * rows)), math.cosh(theta * (total - (d + 1) * rows))
        g = green[own, own].astype(np.float32)
        head = g.astype(ml_dtypes.bfloat16)
        tail = (g - head.astype(np.float32)).astype(ml_dtypes.bfloat16)
        blocks.append(np.concatenate([head, tail, head], axis=1))
        columns = [near[own] / high, far[own] / flow, low * far[own] / norm, fhigh * near[own] / norm]
        vectors.append(np.stack([np.broadcast_to(c[:, None], (rows, 128)) for c in columns]))
        for k in range(1, parts):
            other = d ^ k
            if other < d:
                scalars[d, k] = math.cosh(theta * (other + 1) * rows) / low
            else:
                scalars[d, 4 + k] = math.cosh(theta * (total - other * rows)) / fhigh
    return np.stack(blocks), np.stack(vectors).astype(np.float32), scalars.astype(np.float32)


def call(body, outs, ins, scratch=(), out_space=VMEM):
    return pl.pallas_call(
        body,
        out_shape=[s if hasattr(s, "dtype") else jax.ShapeDtypeStruct(s, F32) for s in outs],
        in_specs=ins,
        out_specs=[out_space] * len(outs),
        scratch_shapes=list(scratch),
        compiler_params=pltpu.CompilerParams(vmem_limit_bytes=24 * 2**20),
    )


def rows_at(start):
    return slice(start, start + STEP)


def sublane(shape):
    return lax.broadcasted_iota(jnp.int32, shape, 0)


def lane(shape):
    return lax.broadcasted_iota(jnp.int32, shape, 1)


def recip(x):
    r = pl.reciprocal(x, approx=True)
    return r * (2.0 - x * r)


def fold(x):
    return sum(x[r : r + 8] for r in range(0, x.shape[0], 8))


def folded(x):
    x = fold(x)
    return sum(x[:, c : c + 128] for c in range(0, x.shape[1], 128))


def lookup(labels, table):
    low = jnp.where(labels == 1, table[1], table[0])
    high = jnp.where(labels == 3, table[3], table[2])
    return jnp.where(labels >= 2, high, low)


def wide(column, width):
    return jnp.concatenate([column] * (width // 128), axis=1)


def ends(value, low, high):
    return jnp.concatenate([value[:, :128] + low, value[:, 128:-128], value[:, -128:] + high], axis=1)


def local(labels, phase_table, collector_mask, collector_value, source):
    nz, ny, nx = labels.shape
    parts = lax.axis_size("gy")
    layers = lax.axis_size("gz")
    block = (nz, ny, nx)
    plane = (1, ny, nx)
    edge = (nz, 8, nx)
    framed = (nz, ny + 16, nx)
    starts = range(0, ny, STEP)
    outer = sorted({0, nz - 1})
    middle = [z for z in range(nz) if z not in outer]
    ends_shape, middle_shape = (len(outer), ny, nx), (len(middle), ny, nx)
    green, vectors, scalars = line_tables(ny * parts, parts)
    green, vectors, scalars = jnp.asarray(green), jnp.asarray(vectors), jnp.asarray(scalars)

    def pick(z, first, second):
        return first.at[outer.index(z)] if z in outer else second.at[middle.index(z)]

    def swap(value, axis, size, partner):
        return lax.ppermute(value, axis, [(i, partner(i) % size) for i in range(size)])

    def inside(value):
        return swap(value, "gz", layers, lambda i: i ^ 1)

    def across(value):
        def partner(i, j):
            k = i + 1 if i % 2 else i - 1
            return (k, j) if 0 <= k < layers else (i, j ^ 1)
        pairs = [(i, j, *partner(i, j)) for i in range(layers) for j in range(parts)]
        return lax.ppermute(value, ALL, [(i * parts + j, k * parts + m) for i, j, k, m in pairs])

    def crosswise(value, step):
        return swap(value, "gy", parts, lambda i: i ^ step)

    def even(axis):
        return lax.axis_index(axis) % 2 == 0

    def borders(labels, in_o, out_o, one_o, three_o, first, last, sems):
        top, bottom = jnp.int32(nz - 1), jnp.int32(0)
        copies = [
            pltpu.make_async_copy(labels.at[pl.ds(jnp.where(even("gz"), top, bottom), 1)], in_o, sems.at[0]),
            pltpu.make_async_copy(labels.at[pl.ds(jnp.where(even("gz"), bottom, top), 1)], out_o, sems.at[1]),
            pltpu.make_async_copy(labels.at[:, pl.ds(0, 8)], first, sems.at[2]),
            pltpu.make_async_copy(labels.at[:, pl.ds(ny - 8, 8)], last, sems.at[3]),
        ]
        for copy in copies:
            copy.start()
        for copy in copies:
            copy.wait()
        for z in range(nz):
            low, high = first[z, 0:1, :], last[z, 7:8, :]
            one_o[z : z + 1, :] = jnp.where(even("gy"), high, low)
            three_o[z : z + 1, :] = jnp.where(even("gy"), low, high)

    sent = [jax.ShapeDtypeStruct(shape, jnp.int32) for shape in (plane, plane, (nz, nx), (nz, nx))]
    in_o, out_o, one, three = call(
        borders, sent, [HBM], [pltpu.VMEM(edge, jnp.int32)] * 2 + [pltpu.SemaphoreType.DMA((4,))]
    )(labels)
    out_o, in_o = across(out_o), inside(in_o)
    one, three = crosswise(one, 1), crosswise(three, 3)

    head = jnp.concatenate([phase_table, collector_value])
    packed = jnp.concatenate(
        [jnp.pad(head, (0, ny - head.shape[0]))[None], collector_mask.reshape(2 * nz, ny).astype(F32)]
    )

    def halves(settings):
        return [wide(settings[n : n + 1, :], nx) for n in range(4)]

    def faces(labels, packed, source, k_o, fx_o, fy_o, fz_o, d_o, e_o, b_o, settings, held, framed_k, sem):
        copy = pltpu.make_async_copy(source, held, sem)
        copy.start()
        for n in range(6):
            value = jnp.broadcast_to(packed[0:1, n : n + 1], (1, 128))
            settings[n : n + 1, :] = 0.5 / value if n < 4 else value
        columns = jnp.transpose(packed[1 : 2 * nz + 1, :])
        table = halves(settings)
        values = [settings[4 + n : 5 + n, :] for n in range(2)]
        for z in range(nz):
            for r in starts:
                k = lookup(labels[z, rows_at(r), :], table)
                k_o[z, rows_at(r), :] = k
                framed_k[z, rows_at(r + 8), :] = k
            framed_k[z, ny + 8 : ny + 16, :] = framed_k[z, ny : ny + 8, :]
            fy_o[z, 0:8, :] = jnp.zeros((8, nx), F32)
        copy.wait()
        sub, across, side = sublane((STEP, nx)), lane((STEP, nx)), lane((STEP, 128))
        for z in range(nz):
            for r in starts:
                at = rows_at(r)
                k = k_o[z, at, :]
                fy = recip(k + framed_k[z, rows_at(r + 9), :])
                if r + STEP == ny:
                    fy = jnp.where(sub == STEP - 1, 0.0, fy)
                fy_o[z, rows_at(r + 8), :] = fy
                fx = jnp.where(across == nx - 1, 0.0, recip(k + pltpu.roll(k, nx - 1, 1)))
                d = fy + fy_o[z, rows_at(r + 7), :] + (fx + pltpu.roll(fx, 1, 1))
                if z > 0:
                    d = d + fz_o[z - 1, at, :]
                if z < nz - 1:
                    fz = recip(k + k_o[z + 1, at, :])
                    fz_o[z, at, :] = fz
                    d = d + fz
                low = jnp.where(side == 0, recip(k[:, :128]) * columns[at, z : z + 1], 0.0)
                high = jnp.where(side == 127, recip(k[:, -128:]) * columns[at, nz + z : nz + z + 1], 0.0)
                e_o[z, at, :] = jnp.concatenate([low, high], axis=1)
                d_o[z, at, :] = ends(d, low, high)
                b_o[z, at, :] = ends(held[z, at, :], low * values[0], high * values[1])
                fx_o[z, at, :] = fx

    k, fx, fy, fz, d, e, b, settings = call(
        faces,
        [block, block, (nz, ny + 8, nx), (nz - 1, ny, nx), block, (nz, ny, 256), block, (8, 128)],
        [VMEM, VMEM, HBM],
        [pltpu.VMEM(block, F32), pltpu.VMEM(framed, F32), pltpu.SemaphoreType.DMA],
    )(labels, packed, source)

    def weighted(x, my, vectors, r, carry):
        return (
            carry[0] + fold(x * wide(vectors[my, 0, rows_at(r), :], nx)),
            carry[1] + fold(x * wide(vectors[my, 1, rows_at(r), :], nx)),
        )

    def sums_out(my, sums, z, outs):
        right, left = (jnp.sum(v, 0, keepdims=True) for v in sums)
        for step, out in enumerate(outs, 1):
            out[z : z + 1, :] = jnp.where((my ^ step) > my, right, left)

    zero = lambda: jnp.zeros((8, nx), F32)
    none = lambda: jnp.zeros((8, 128), F32)

    def scaled(settings, k, y_one, y_three, z_in, z_out, d, b, vectors, s_o, xo_o, xm_o, fye_o, fze_o, one, two, three):
        my, level = lax.axis_index("gy"), lax.axis_index("gz")
        has_low, has_high = (my > 0).astype(F32), (my < parts - 1).astype(F32)
        has_below, has_above = (level > 0).astype(F32), (level < layers - 1).astype(F32)
        sub = sublane((STEP, nx))
        table = halves(settings)
        for z in range(nz):
            ones, threes = y_one[z : z + 1, :], y_three[z : z + 1, :]
            ylo, yhi = jnp.where(even("gy"), threes, ones), jnp.where(even("gy"), ones, threes)
            first = has_low * recip(lookup(ylo, table) + k[z, 0:1, :])
            last = has_high * recip(lookup(yhi, table) + k[z, ny - 1 : ny, :])
            fye_o[z, 0:1, :] = first
            fye_o[z, 1:2, :] = last
            carry = (zero(), zero())
            for r in starts:
                at = rows_at(r)
                diagonal = d[z, at, :]
                if r == 0:
                    diagonal = diagonal + jnp.where(sub == 0, first, 0.0)
                if r + STEP == ny:
                    diagonal = diagonal + jnp.where(sub == STEP - 1, last, 0.0)
                if z == 0:
                    face = has_below * recip(lookup(jnp.where(even("gz"), z_out[0, at, :], z_in[0, at, :]), table) + k[z, at, :])
                    fze_o[0, at, :] = face
                    diagonal = diagonal + face
                if z == nz - 1:
                    face = has_above * recip(lookup(jnp.where(even("gz"), z_in[0, at, :], z_out[0, at, :]), table) + k[z, at, :])
                    fze_o[1, at, :] = face
                    diagonal = diagonal + face
                s = lax.rsqrt(diagonal)
                x = s * b[z, at, :]
                s_o[z, at, :] = s
                pick(z, xo_o, xm_o)[at, :] = x
                carry = weighted(x, my, vectors, r, carry)
            sums_out(my, carry, z, (one, two, three))
            low, high = s_o[z, 0:1, :], s_o[z, ny - 1 : ny, :]
            one[nz + z : nz + z + 1, :] = jnp.where(even("gy"), high, low)
            three[nz + z : nz + z + 1, :] = jnp.where(even("gy"), low, high)

    s, xo, xm, fye, fze, one, two, three = call(
        scaled,
        [block, ends_shape, middle_shape, edge, (2, ny, nx), (2 * nz, nx), (nz, nx), (2 * nz, nx)],
        [VMEM] * 9,
    )(settings, k, one, three, in_o, out_o, d, b, vectors)

    def lines(xo, xm, green, out):
        my = lax.axis_index("gy")
        for z in range(nz):
            x = pick(z, xo, xm)[...]
            head = x.astype(jnp.bfloat16)
            tail = (x - head.astype(F32)).astype(jnp.bfloat16)
            stack = jnp.concatenate([head, head, tail], axis=0)
            out[z] = jnp.dot(green[my], stack, preferred_element_type=F32)

    def solve(z, part, s, xo, xm, vectors, scalars, one, two, three, s_one, s_three, put):
        my = lax.axis_index("gy")
        got = [r[z : z + 1, :] for r in (one, two, three)]
        left = sum(scalars[my, n + 1] * got[n] for n in range(3))
        right = sum(scalars[my, 5 + n] * got[n] for n in range(3))
        ones, threes = s_one[nz + z : nz + z + 1, :], s_three[nz + z : nz + z + 1, :]
        for r in starts:
            at = rows_at(r)
            g = part[z, at, :] + (wide(vectors[my, 2, at, :], nx) * left + wide(vectors[my, 3, at, :], nx) * right)
            put(r + 8, s[z, at, :] * g)
            if r == 0:
                beside = (2.0 + SHIFT) * g[0:1] - g[1:2] - pick(z, xo, xm)[0:1, :]
                put(7, jnp.where(even("gy"), threes, ones) * beside)
            if r + STEP == ny:
                beside = (2.0 + SHIFT) * g[-1:] - g[-2:-1] - pick(z, xo, xm)[ny - 1 : ny, :]
                put(ny + 8, jnp.where(even("gy"), ones, threes) * beside)

    def solve_outer(part, s, xo, xm, vectors, scalars, one, two, three, s_one, s_three, p_o, in_o, out_o):
        for n, z in enumerate(outer):
            def put(r, value):
                p_o[n, r : r + value.shape[0], :] = value
            solve(z, part, s, xo, xm, vectors, scalars, one, two, three, s_one, s_three, put)
        top = jnp.where(even("gz"), 1, 0)
        for r in starts:
            in_o[0, rows_at(r), :] = p_o[top, rows_at(r + 8), :]
            out_o[0, rows_at(r), :] = p_o[1 - top, rows_at(r + 8), :]

    def total(value):
        return jnp.sum(jnp.sum(value, 0, keepdims=True), 1, keepdims=True)

    def dots_out(out, sums, first):
        at = lane((1, 128))
        row = jnp.zeros((1, 128), F32)
        for n, value in enumerate(sums, first):
            row = jnp.where(at == n, total(value), row)
        out[...] = row

    def operator(read, z, r, fx, fy, fz, fye, e):
        at = rows_at(r)
        v = read(z, r + 8)
        q = fy[z, rows_at(r + 8), :] * (v - read(z, r + 9)) + fy[z, rows_at(r + 7), :] * (v - read(z, r + 7))
        sub = sublane((STEP, nx))
        if r == 0:
            q = q + jnp.where(sub == 0, fye[z, 0:1, :], 0.0) * (v - read(z, r + 7))
        if r + STEP == ny:
            q = q + jnp.where(sub == STEP - 1, fye[z, 1:2, :], 0.0) * (v - read(z, r + 9))
        flow = fx[z, at, :] * (v - pltpu.roll(v, nx - 1, 1))
        q = q + (flow - pltpu.roll(flow, 1, 1))
        if z > 0:
            q = q + fz[z - 1, at, :] * (v - read(z - 1, r + 8))
        if z < nz - 1:
            q = q + fz[z, at, :] * (v - read(z + 1, r + 8))
        edges = e[z, at, :]
        return v, ends(q, edges[:, :128] * v[:, :128], edges[:, 128:] * v[:, -128:])

    def fill(part, s, xo, xm, vectors, scalars, one, two, three, s_one, s_three, p_outer, p_o, field):
        for z in middle:
            def put(r, value):
                field[z, r : r + value.shape[0], :] = value
                if value.shape[0] == STEP:
                    p_o[z, rows_at(r - 8), :] = value
            solve(z, part, s, xo, xm, vectors, scalars, one, two, three, s_one, s_three, put)
        for n, z in enumerate(outer):
            for r in starts:
                p_o[z, rows_at(r), :] = p_outer[n, rows_at(r + 8), :]

        def read(z, r):
            return p_outer[outer.index(z), rows_at(r), :] if z in outer else field[z, rows_at(r), :]
        return read

    def inner_first(part, s, xo, xm, vectors, scalars, one, two, three, s_one, s_three, p_outer, fx, fy, fz, fye, e, b,
                    p_o, q_o, xm_o, one_o, two_o, three_o, dots, field):
        my = lax.axis_index("gy")
        read = fill(part, s, xo, xm, vectors, scalars, one, two, three, s_one, s_three, p_outer, p_o, field)
        bp, pq = none(), none()
        for z in outer + middle:
            carry = (zero(), zero())
            for r in starts:
                at = rows_at(r)
                v, image = operator(read, z, r, fx, fy, fz, fye, e)
                bp = bp + folded(b[z, at, :] * v)
                q_o[z, at, :] = image
                if z in middle:
                    scaled_image = s[z, at, :] * image
                    xm_o[middle.index(z), at, :] = scaled_image
                    carry = weighted(scaled_image, my, vectors, r, carry)
                    pq = pq + folded(v * image)
            if z in middle:
                sums_out(my, carry, z, (one_o, two_o, three_o))
        dots_out(dots, (bp, pq), 0)

    def image_of(z, ends, whole, at):
        return ends[outer.index(z), at, :] if z in outer else whole[z, at, :]

    def outside(z, r, v, image, z_in, z_out, fze):
        at = rows_at(r)
        if z == 0:
            image = image + fze[0, at, :] * (v - jnp.where(even("gz"), z_out[0, at, :], z_in[0, at, :]))
        if z == nz - 1:
            image = image + fze[1, at, :] * (v - jnp.where(even("gz"), z_in[0, at, :], z_out[0, at, :]))
        return image

    def outer_first(p, q, one, two, three, z_in, z_out, fze, s, vectors, dots, qo_o, xo_o, one_o, two_o, three_o, dots_o):
        my = lax.axis_index("gy")
        pq = none()
        for z in outer:
            carry = (zero(), zero())
            for r in starts:
                at = rows_at(r)
                v = p[z, at, :]
                image = outside(z, r, v, q[z, at, :], z_in, z_out, fze)
                scaled_image = s[z, at, :] * image
                qo_o[outer.index(z), at, :] = image
                xo_o[outer.index(z), at, :] = scaled_image
                carry = weighted(scaled_image, my, vectors, r, carry)
                pq = pq + folded(v * image)
            sums_out(my, carry, z, (one_o, two_o, three_o))
        for z in middle:
            for got, out in ((one, one_o), (two, two_o), (three, three_o)):
                out[z : z + 1, :] = got[z : z + 1, :]
        dots_out(dots_o, (none(), pq), 0)
        dots_o[...] = dots_o[...] + dots[...]

    def inner_last(part, s, xo, xm, vectors, scalars, one, two, three, s_one, s_three, p_outer, fx, fy, fz, fye, e, b, q, qo,
                   w_o, v_o, dots, field):
        read = fill(part, s, xo, xm, vectors, scalars, one, two, three, s_one, s_three, p_outer, w_o, field)
        bw, qw, wv = none(), none(), none()
        for z in range(nz):
            for r in starts:
                at = rows_at(r)
                w, image = operator(read, z, r, fx, fy, fz, fye, e)
                bw = bw + folded(b[z, at, :] * w)
                qw = qw + folded(image_of(z, qo, q, at) * w)
                wv = wv + folded(image * w)
                v_o[z, at, :] = image
        dots_out(dots, (bw, qw, wv), 2)

    def outer_last(w, v, z_in, z_out, fze, dots_first, dots, v_o, dots_o):
        wv = none()
        for n, z in enumerate(outer):
            for r in starts:
                at = rows_at(r)
                field, image = w[z, at, :], v[z, at, :]
                full = outside(z, r, field, image, z_in, z_out, fze)
                v_o[n, at, :] = full
                wv = wv + folded((full - image) * field)
        dots_out(dots_o, (wv,), 4)
        dots_o[...] = dots_o[...] + (dots[...] + dots_first[...])

    def combine(gathered, p, w, q, qo, v, vo, b, x_o, r_o, x_held, r_held, sems):
        sums = jnp.sum(gathered[...], 0, keepdims=True)
        at = lane((1, 128))
        bp, pq, bw, qw, wv = (jnp.sum(jnp.where(at == n, sums, 0.0), 1, keepdims=True) for n in range(5))
        step = bp / pq
        product = bp - step * (bw + pq) + step * step * qw
        more = 1.0 + product / bp
        curvature = more * more * pq - 2.0 * more * step * qw + step * step * wv
        second = product / curvature
        along = jnp.broadcast_to(step + second * more, (STEP, nx))
        across = jnp.broadcast_to(second * step, (STEP, nx))
        copies = []
        for z in range(nz):
            for r in starts:
                at = rows_at(r)
                x_held[z, at, :] = along * p[z, at, :] - across * w[z, at, :]
                r_held[z, at, :] = b[z, at, :] - along * image_of(z, qo, q, at) + across * image_of(z, vo, v, at)
            for n, (held, out) in enumerate(((x_held, x_o), (r_held, r_o))):
                copies.append(pltpu.make_async_copy(held.at[z], out.at[z], sems.at[n, z]))
                copies[-1].start()
        for copy in copies:
            copy.wait()

    def gather(sums):
        return [crosswise(v, n) for n, v in enumerate(sums, 1)]

    field = [pltpu.VMEM(framed, F32)]
    rows = [(nz, nx)] * 3
    framed_pair = (len(outer), ny + 16, nx)

    def start(xo, xm, sums, beside):
        got = gather(sums)
        beside = beside or (got[0], got[2])
        part = call(lines, [block], [VMEM] * 3)(xo, xm, green)[0]
        known = (part, s, xo, xm, vectors, scalars, *got, *beside)
        pair, in_o, out_o = call(solve_outer, [framed_pair, plane, plane], places)(*known)
        out_o = across(out_o)
        return (*known, pair), inside(in_o), out_o, beside

    places = [VMEM] * 5 + [SMEM] + [VMEM] * 5
    known, z_in, z_out, beside = start(xo, xm, (one, two, three), None)
    p, q, xm, *sums, dots = call(
        inner_first, [block, block, middle_shape, *rows, (1, 128)], places + [VMEM] * 7, field
    )(*known, fx, fy, fz, fye, e, b)
    qo, xo, *sums, dots = call(outer_first, [ends_shape, ends_shape, *rows, (1, 128)], [VMEM] * 11)(
        p, q, *sums, z_in, z_out, fze, s, vectors, dots
    )
    known, z_in, z_out, _ = start(xo, xm, sums, beside)
    w, v, last_dots = call(inner_last, [block, block, (1, 128)], places + [VMEM] * 9, field)(
        *known, fx, fy, fz, fye, e, b, q, qo
    )
    vo, dots = call(outer_last, [ends_shape, (1, 128)], [VMEM] * 7)(w, v, z_in, z_out, fze, last_dots, dots)
    count = parts * layers
    gathered = lax.all_to_all(jnp.broadcast_to(dots, (count, 128)), ALL, 0, 0, tiled=True)
    return tuple(
        call(
            combine,
            [block, block],
            [VMEM] * 8,
            [pltpu.VMEM(block, F32)] * 2 + [pltpu.SemaphoreType.DMA((2, nz))],
            out_space=HBM,
        )(gathered, p, w, q, qo, v, vo, b)
    )


def solution(mesh):
    return jax.shard_map(
        local,
        mesh=mesh,
        in_specs=(P("gz", "gy", None), P(), P(None, "gz", "gy"), P(), P("gz", "gy", None)),
        out_specs=(P("gz", "gy", None), P("gz", "gy", None)),
        check_vma=False,
    )
```

```python
import math

import jax
import jax.numpy as jnp
import ml_dtypes
import numpy as np
from jax import lax
from jax.experimental import pallas as pl
from jax.experimental.pallas import tpu as pltpu
from jax.sharding import PartitionSpec as P

F32 = jnp.float32
SHIFT = 0.0016
VMEM = pl.BlockSpec(memory_space=pltpu.VMEM)
HBM = pl.BlockSpec(memory_space=pltpu.HBM)
ALL = ("gz", "gy")
STEP = 64


def line_tables(total, parts):
    rows = total // parts
    theta = math.acosh(1.0 + SHIFT / 2.0)
    near = np.cosh(theta * (np.arange(total) + 0.5))
    far = near[::-1]
    norm = math.sinh(theta) * math.sinh(total * theta)
    at = np.arange(total)
    green = np.where(at[:, None] <= at[None, :], near[:, None] * far[None, :], far[:, None] * near[None, :]) / norm
    blocks, vectors, scalars = [], [], np.zeros((parts, 8))
    for d in range(parts):
        own = slice(d * rows, (d + 1) * rows)
        low, high = math.cosh(theta * d * rows), math.cosh(theta * (d + 1) * rows)
        flow, fhigh = math.cosh(theta * (total - d * rows)), math.cosh(theta * (total - (d + 1) * rows))
        g = green[own, own].astype(np.float32)
        head = g.astype(ml_dtypes.bfloat16)
        tail = (g - head.astype(np.float32)).astype(ml_dtypes.bfloat16)
        blocks.append(np.concatenate([head, tail, head], axis=1))
        columns = [near[own] / high, far[own] / flow, low * far[own] / norm, fhigh * near[own] / norm]
        vectors.append(np.stack([np.broadcast_to(c[:, None], (rows, 128)) for c in columns]))
        for k in range(1, parts):
            other = d ^ k
            if other < d:
                scalars[d, k] = math.cosh(theta * (other + 1) * rows) / low
            else:
                scalars[d, 4 + k] = math.cosh(theta * (total - other * rows)) / fhigh
    return np.stack(blocks), np.stack(vectors).astype(np.float32), np.repeat(scalars[..., None], 128, 2).astype(np.float32)


def call(body, outs, ins, scratch=(), out_space=VMEM):
    return pl.pallas_call(
        body,
        out_shape=[s if hasattr(s, "dtype") else jax.ShapeDtypeStruct(s, F32) for s in outs],
        in_specs=ins,
        out_specs=[out_space] * len(outs),
        scratch_shapes=list(scratch),
        compiler_params=pltpu.CompilerParams(vmem_limit_bytes=24 * 2**20),
    )


def rows_at(start):
    return slice(start, start + STEP)


def sublane(shape):
    return lax.broadcasted_iota(jnp.int32, shape, 0)


def lane(shape):
    return lax.broadcasted_iota(jnp.int32, shape, 1)


def recip(x):
    r = pl.reciprocal(x, approx=True)
    return r * (2.0 - x * r)


def fold(x):
    return sum(x[r : r + 8] for r in range(0, x.shape[0], 8))


def folded(x):
    x = fold(x)
    return sum(x[:, c : c + 128] for c in range(0, x.shape[1], 128))


def lookup(labels, table):
    low = jnp.where(labels == 1, table[1], table[0])
    high = jnp.where(labels == 3, table[3], table[2])
    return jnp.where(labels >= 2, high, low)


def wide(column, width):
    return jnp.concatenate([column] * (width // 128), axis=1)


def ends(value, low, high):
    return jnp.concatenate([value[:, :128] + low, value[:, 128:-128], value[:, -128:] + high], axis=1)


def local(labels, phase_table, collector_mask, collector_value, source):
    nz, ny, nx = labels.shape
    parts = lax.axis_size("gy")
    layers = lax.axis_size("gz")
    block = (nz, ny, nx)
    plane = (1, ny, nx)
    edge = (nz, 8, nx)
    framed = (nz, ny + 16, nx)
    starts = range(0, ny, STEP)
    outer = sorted({0, nz - 1})
    middle = [z for z in range(nz) if z not in outer]
    ends_shape, middle_shape = (len(outer), ny, nx), (len(middle), ny, nx)
    green, vectors, scalars = line_tables(ny * parts, parts)
    green, vectors, scalars = jnp.asarray(green), jnp.asarray(vectors), jnp.asarray(scalars)

    def pick(z, first, second):
        return first.at[outer.index(z)] if z in outer else second.at[middle.index(z)]

    def swap(value, axis, size, partner):
        return lax.ppermute(value, axis, [(i, partner(i) % size) for i in range(size)])

    def inside(value):
        return swap(value, "gz", layers, lambda i: i ^ 1)

    def across(value):
        def partner(i, j):
            k = i + 1 if i % 2 else i - 1
            return (k, j) if 0 <= k < layers else (i, j ^ 1)
        pairs = [(i, j, *partner(i, j)) for i in range(layers) for j in range(parts)]
        return lax.ppermute(value, ALL, [(i * parts + j, k * parts + m) for i, j, k, m in pairs])

    def crosswise(value, step):
        return swap(value, "gy", parts, lambda i: i ^ step)

    def even(axis):
        return lax.axis_index(axis) % 2 == 0

    def side(inner):
        return jnp.where(even("gz") == inner, jnp.int32(nz - 1), jnp.int32(0))

    def border(labels, out_o, sem):
        copy = pltpu.make_async_copy(labels.at[pl.ds(side(False), 1)], out_o, sem)
        copy.start()
        copy.wait()

    def borders(labels, in_o, one_o, three_o, first, last, sems):
        copies = [
            pltpu.make_async_copy(labels.at[pl.ds(side(True), 1)], in_o, sems.at[0]),
            pltpu.make_async_copy(labels.at[:, pl.ds(0, 8)], first, sems.at[1]),
            pltpu.make_async_copy(labels.at[:, pl.ds(ny - 8, 8)], last, sems.at[2]),
        ]
        for copy in copies:
            copy.start()
        for copy in copies:
            copy.wait()
        for z in range(nz):
            low, high = first[z, 0:1, :], last[z, 7:8, :]
            one_o[z : z + 1, :] = jnp.where(even("gy"), high, low)
            three_o[z : z + 1, :] = jnp.where(even("gy"), low, high)

    sent = [jax.ShapeDtypeStruct(shape, jnp.int32) for shape in (plane, (nz, nx), (nz, nx))]
    out_o = call(border, sent[:1], [HBM], [pltpu.SemaphoreType.DMA])(labels)[0]
    in_o, one, three = call(
        borders, sent, [HBM], [pltpu.VMEM(edge, jnp.int32)] * 2 + [pltpu.SemaphoreType.DMA((3,))]
    )(labels)
    out_o, in_o = across(out_o), inside(in_o)
    one, three = crosswise(one, 1), crosswise(three, 3)

    head = jnp.concatenate([phase_table, collector_value])
    packed = jnp.concatenate(
        [jnp.pad(head, (0, ny - head.shape[0]))[None], collector_mask.reshape(2 * nz, ny).astype(F32)]
    )

    def halves(settings):
        return [wide(settings[n : n + 1, :], nx) for n in range(4)]

    def faces(labels, packed, source, k_o, fx_o, fy_o, fz_o, d_o, e_o, b_o, settings, held, framed_k, sem):
        copy = pltpu.make_async_copy(source, held, sem)
        copy.start()
        for n in range(6):
            value = jnp.broadcast_to(packed[0:1, n : n + 1], (1, 128))
            settings[n : n + 1, :] = 0.5 / value if n < 4 else value
        columns = jnp.transpose(packed[1 : 2 * nz + 1, :])
        table = halves(settings)
        values = [settings[4 + n : 5 + n, :] for n in range(2)]
        for z in range(nz):
            for r in starts:
                k = lookup(labels[z, rows_at(r), :], table)
                k_o[z, rows_at(r), :] = k
                framed_k[z, rows_at(r + 8), :] = k
            framed_k[z, ny + 8 : ny + 16, :] = framed_k[z, ny : ny + 8, :]
            fy_o[z, 0:8, :] = jnp.zeros((8, nx), F32)
        copy.wait()
        sub, across, side = sublane((STEP, nx)), lane((STEP, nx)), lane((STEP, 128))
        for z in range(nz):
            for r in starts:
                at = rows_at(r)
                k = k_o[z, at, :]
                fy = recip(k + framed_k[z, rows_at(r + 9), :])
                if r + STEP == ny:
                    fy = jnp.where(sub == STEP - 1, 0.0, fy)
                fy_o[z, rows_at(r + 8), :] = fy
                fx = jnp.where(across == nx - 1, 0.0, recip(k + pltpu.roll(k, nx - 1, 1)))
                d = fy + fy_o[z, rows_at(r + 7), :] + (fx + pltpu.roll(fx, 1, 1))
                if z > 0:
                    d = d + fz_o[z - 1, at, :]
                if z < nz - 1:
                    fz = recip(k + k_o[z + 1, at, :])
                    fz_o[z, at, :] = fz
                    d = d + fz
                low = jnp.where(side == 0, recip(k[:, :128]) * columns[at, z : z + 1], 0.0)
                high = jnp.where(side == 127, recip(k[:, -128:]) * columns[at, nz + z : nz + z + 1], 0.0)
                e_o[z, at, :] = jnp.concatenate([low, high], axis=1)
                d_o[z, at, :] = ends(d, low, high)
                b_o[z, at, :] = ends(held[z, at, :], low * values[0], high * values[1])
                fx_o[z, at, :] = fx

    k, fx, fy, fz, d, e, b, settings = call(
        faces,
        [block, block, (nz, ny + 8, nx), (nz - 1, ny, nx), block, (nz, ny, 256), block, (8, 128)],
        [VMEM, VMEM, HBM],
        [pltpu.VMEM(block, F32), pltpu.VMEM(framed, F32), pltpu.SemaphoreType.DMA],
    )(labels, packed, source)

    def weighted(x, my, vectors, r, carry):
        return (
            carry[0] + fold(x * wide(vectors[my, 0, rows_at(r), :], nx)),
            carry[1] + fold(x * wide(vectors[my, 1, rows_at(r), :], nx)),
        )

    def sums_out(my, sums, z, outs):
        right, left = (jnp.sum(v, 0, keepdims=True) for v in sums)
        for step, out in enumerate(outs, 1):
            out[z : z + 1, :] = jnp.where((my ^ step) > my, right, left)

    zero = lambda: jnp.zeros((8, nx), F32)
    none = lambda: jnp.zeros((8, 128), F32)

    def scaled(settings, k, y_one, y_three, z_in, z_out, d, b, vectors, s_o, xo_o, xm_o, fye_o, fze_o, one, two, three):
        my, level = lax.axis_index("gy"), lax.axis_index("gz")
        has_low, has_high = (my > 0).astype(F32), (my < parts - 1).astype(F32)
        has_below, has_above = (level > 0).astype(F32), (level < layers - 1).astype(F32)
        sub = sublane((STEP, nx))
        table = halves(settings)
        for z in range(nz):
            ones, threes = y_one[z : z + 1, :], y_three[z : z + 1, :]
            ylo, yhi = jnp.where(even("gy"), threes, ones), jnp.where(even("gy"), ones, threes)
            first = has_low * recip(lookup(ylo, table) + k[z, 0:1, :])
            last = has_high * recip(lookup(yhi, table) + k[z, ny - 1 : ny, :])
            fye_o[z, 0:1, :] = first
            fye_o[z, 1:2, :] = last
            carry = (zero(), zero())
            for r in starts:
                at = rows_at(r)
                diagonal = d[z, at, :]
                if r == 0:
                    diagonal = diagonal + jnp.where(sub == 0, first, 0.0)
                if r + STEP == ny:
                    diagonal = diagonal + jnp.where(sub == STEP - 1, last, 0.0)
                if z == 0:
                    face = has_below * recip(lookup(jnp.where(even("gz"), z_out[0, at, :], z_in[0, at, :]), table) + k[z, at, :])
                    fze_o[0, at, :] = face
                    diagonal = diagonal + face
                if z == nz - 1:
                    face = has_above * recip(lookup(jnp.where(even("gz"), z_in[0, at, :], z_out[0, at, :]), table) + k[z, at, :])
                    fze_o[1, at, :] = face
                    diagonal = diagonal + face
                s = lax.rsqrt(diagonal)
                x = s * b[z, at, :]
                s_o[z, at, :] = s
                pick(z, xo_o, xm_o)[at, :] = x
                carry = weighted(x, my, vectors, r, carry)
            sums_out(my, carry, z, (one, two, three))
            low, high = s_o[z, 0:1, :], s_o[z, ny - 1 : ny, :]
            one[nz + z : nz + z + 1, :] = jnp.where(even("gy"), high, low)
            three[nz + z : nz + z + 1, :] = jnp.where(even("gy"), low, high)

    s, xo, xm, fye, fze, one, two, three = call(
        scaled,
        [block, ends_shape, middle_shape, edge, (2, ny, nx), (2 * nz, nx), (nz, nx), (2 * nz, nx)],
        [VMEM] * 9,
    )(settings, k, one, three, in_o, out_o, d, b, vectors)

    def lines(xo, xm, green, out):
        my = lax.axis_index("gy")
        for z in range(nz):
            x = pick(z, xo, xm)[...]
            head = x.astype(jnp.bfloat16)
            tail = (x - head.astype(F32)).astype(jnp.bfloat16)
            stack = jnp.concatenate([head, head, tail], axis=0)
            out[z] = jnp.dot(green[my], stack, preferred_element_type=F32)

    def solve(z, x, part, s, vectors, scalars, one, two, three, s_one, s_three, put):
        my = lax.axis_index("gy")
        got = [r[pl.ds(z, 1), :] for r in (one, two, three)]
        left = sum(wide(scalars[my, n + 1 : n + 2, :], nx) * got[n] for n in range(3))
        right = sum(wide(scalars[my, n + 5 : n + 6, :], nx) * got[n] for n in range(3))
        ones, threes = s_one[pl.ds(nz + z, 1), :], s_three[pl.ds(nz + z, 1), :]
        for r in starts:
            at = rows_at(r)
            g = part[z, at, :] + (wide(vectors[my, 2, at, :], nx) * left + wide(vectors[my, 3, at, :], nx) * right)
            put(r + 8, s[z, at, :] * g)
            if r == 0:
                beside = (2.0 + SHIFT) * g[0:1] - g[1:2] - x[0:1, :]
                put(7, jnp.where(even("gy"), threes, ones) * beside)
            if r + STEP == ny:
                beside = (2.0 + SHIFT) * g[-1:] - g[-2:-1] - x[ny - 1 : ny, :]
                put(ny + 8, jnp.where(even("gy"), ones, threes) * beside)

    def solve_out(part, s, xo, xm, vectors, scalars, one, two, three, s_one, s_three, held_o, out_o):
        def put(r, value):
            held_o[r : r + value.shape[0], :] = value
            if value.shape[0] == STEP:
                out_o[0, rows_at(r - 8), :] = value
        z = side(False)
        place = xo.at[jnp.where(z == 0, 0, 1)]
        solve(z, place, part, s, vectors, scalars, one, two, three, s_one, s_three, put)

    def solve_in(part, s, xo, xm, vectors, scalars, one, two, three, s_one, s_three, held, p_o, in_o):
        z = side(True)
        n = jnp.where(z == 0, 0, 1)

        def put(r, value):
            p_o[n, r : r + value.shape[0], :] = value
            if value.shape[0] == STEP:
                in_o[0, rows_at(r - 8), :] = value
        solve(z, xo.at[n], part, s, vectors, scalars, one, two, three, s_one, s_three, put)
        for r in range(0, ny + 16, 16):
            p_o[1 - n, r : r + 16, :] = held[r : r + 16, :]

    def total(value):
        return jnp.sum(jnp.sum(value, 0, keepdims=True), 1, keepdims=True)

    def dots_out(out, sums, first):
        at = lane((1, 128))
        row = jnp.zeros((1, 128), F32)
        for n, value in enumerate(sums, first):
            row = jnp.where(at == n, total(value), row)
        out[...] = row

    def operator(read, z, r, fx, fy, fz, fye, e):
        at = rows_at(r)
        v = read(z, r + 8)
        q = fy[z, rows_at(r + 8), :] * (v - read(z, r + 9)) + fy[z, rows_at(r + 7), :] * (v - read(z, r + 7))
        sub = sublane((STEP, nx))
        if r == 0:
            q = q + jnp.where(sub == 0, fye[z, 0:1, :], 0.0) * (v - read(z, r + 7))
        if r + STEP == ny:
            q = q + jnp.where(sub == STEP - 1, fye[z, 1:2, :], 0.0) * (v - read(z, r + 9))
        flow = fx[z, at, :] * (v - pltpu.roll(v, nx - 1, 1))
        q = q + (flow - pltpu.roll(flow, 1, 1))
        if z > 0:
            q = q + fz[z - 1, at, :] * (v - read(z - 1, r + 8))
        if z < nz - 1:
            q = q + fz[z, at, :] * (v - read(z + 1, r + 8))
        edges = e[z, at, :]
        return v, ends(q, edges[:, :128] * v[:, :128], edges[:, 128:] * v[:, -128:])

    def fill(part, s, xo, xm, vectors, scalars, one, two, three, s_one, s_three, p_outer, p_o, field):
        for z in middle:
            def put(r, value):
                field[z, r : r + value.shape[0], :] = value
                if value.shape[0] == STEP:
                    p_o[z, rows_at(r - 8), :] = value
            solve(z, pick(z, xo, xm), part, s, vectors, scalars, one, two, three, s_one, s_three, put)
        for n, z in enumerate(outer):
            for r in starts:
                p_o[z, rows_at(r), :] = p_outer[n, rows_at(r + 8), :]

        def read(z, r):
            return p_outer[outer.index(z), rows_at(r), :] if z in outer else field[z, rows_at(r), :]
        return read

    def inner_first(part, s, xo, xm, vectors, scalars, one, two, three, s_one, s_three, p_outer, fx, fy, fz, fye, e, b,
                    p_o, q_o, xm_o, one_o, two_o, three_o, dots, field):
        my = lax.axis_index("gy")
        read = fill(part, s, xo, xm, vectors, scalars, one, two, three, s_one, s_three, p_outer, p_o, field)
        bp, pq = none(), none()
        for z in outer + middle:
            carry = (zero(), zero())
            for r in starts:
                at = rows_at(r)
                v, image = operator(read, z, r, fx, fy, fz, fye, e)
                bp = bp + folded(b[z, at, :] * v)
                q_o[z, at, :] = image
                if z in middle:
                    scaled_image = s[z, at, :] * image
                    xm_o[middle.index(z), at, :] = scaled_image
                    carry = weighted(scaled_image, my, vectors, r, carry)
                    pq = pq + folded(v * image)
            if z in middle:
                sums_out(my, carry, z, (one_o, two_o, three_o))
        dots_out(dots, (bp, pq), 0)

    def image_of(z, ends, whole, at):
        return ends[outer.index(z), at, :] if z in outer else whole[z, at, :]

    def outside(z, r, v, image, z_in, z_out, fze):
        at = rows_at(r)
        if z == 0:
            image = image + fze[0, at, :] * (v - jnp.where(even("gz"), z_out[0, at, :], z_in[0, at, :]))
        if z == nz - 1:
            image = image + fze[1, at, :] * (v - jnp.where(even("gz"), z_in[0, at, :], z_out[0, at, :]))
        return image

    def outer_first(p, q, one, two, three, z_in, z_out, fze, s, vectors, dots, qo_o, xo_o, one_o, two_o, three_o, dots_o):
        my = lax.axis_index("gy")
        pq = none()
        for z in outer:
            carry = (zero(), zero())
            for r in starts:
                at = rows_at(r)
                v = p[z, at, :]
                image = outside(z, r, v, q[z, at, :], z_in, z_out, fze)
                scaled_image = s[z, at, :] * image
                qo_o[outer.index(z), at, :] = image
                xo_o[outer.index(z), at, :] = scaled_image
                carry = weighted(scaled_image, my, vectors, r, carry)
                pq = pq + folded(v * image)
            sums_out(my, carry, z, (one_o, two_o, three_o))
        for z in middle:
            for got, out in ((one, one_o), (two, two_o), (three, three_o)):
                out[z : z + 1, :] = got[z : z + 1, :]
        dots_out(dots_o, (none(), pq), 0)
        dots_o[...] = dots_o[...] + dots[...]

    def inner_last(part, s, xo, xm, vectors, scalars, one, two, three, s_one, s_three, p_outer, fx, fy, fz, fye, e, b, q, qo,
                   w_o, v_o, dots, field):
        read = fill(part, s, xo, xm, vectors, scalars, one, two, three, s_one, s_three, p_outer, w_o, field)
        bw, qw, wv = none(), none(), none()
        for z in range(nz):
            for r in starts:
                at = rows_at(r)
                w, image = operator(read, z, r, fx, fy, fz, fye, e)
                bw = bw + folded(b[z, at, :] * w)
                qw = qw + folded(image_of(z, qo, q, at) * w)
                wv = wv + folded(image * w)
                v_o[z, at, :] = image
        dots_out(dots, (bw, qw, wv), 2)

    def outer_last(w, v, z_in, z_out, fze, dots_first, dots, v_o, dots_o):
        wv = none()
        for n, z in enumerate(outer):
            for r in starts:
                at = rows_at(r)
                field, image = w[z, at, :], v[z, at, :]
                full = outside(z, r, field, image, z_in, z_out, fze)
                v_o[n, at, :] = full
                wv = wv + folded((full - image) * field)
        dots_out(dots_o, (wv,), 4)
        dots_o[...] = dots_o[...] + (dots[...] + dots_first[...])

    def combine(gathered, p, w, q, qo, v, vo, b, x_o, r_o, x_held, r_held, sems):
        sums = jnp.sum(gathered[...], 0, keepdims=True)
        at = lane((1, 128))
        bp, pq, bw, qw, wv = (jnp.sum(jnp.where(at == n, sums, 0.0), 1, keepdims=True) for n in range(5))
        step = bp / pq
        product = bp - step * (bw + pq) + step * step * qw
        more = 1.0 + product / bp
        curvature = more * more * pq - 2.0 * more * step * qw + step * step * wv
        second = product / curvature
        along = jnp.broadcast_to(step + second * more, (STEP, nx))
        across = jnp.broadcast_to(second * step, (STEP, nx))
        copies = []
        for z in range(nz):
            for r in starts:
                at = rows_at(r)
                x_held[z, at, :] = along * p[z, at, :] - across * w[z, at, :]
                r_held[z, at, :] = b[z, at, :] - along * image_of(z, qo, q, at) + across * image_of(z, vo, v, at)
            for n, (held, out) in enumerate(((x_held, x_o), (r_held, r_o))):
                copies.append(pltpu.make_async_copy(held.at[z], out.at[z], sems.at[n, z]))
                copies[-1].start()
        for copy in copies:
            copy.wait()

    def gather(sums):
        return [crosswise(v, n) for n, v in enumerate(sums, 1)]

    field = [pltpu.VMEM(framed, F32)]
    rows = [(nz, nx)] * 3
    framed_pair = (len(outer), ny + 16, nx)

    places = [VMEM] * 12

    def start(xo, xm, sums, beside):
        got = gather(sums)
        beside = beside or (got[0], got[2])
        part = call(lines, [block], [VMEM] * 3)(xo, xm, green)[0]
        known = (part, s, xo, xm, vectors, scalars, *got, *beside)
        held, out_o = call(solve_out, [(ny + 16, nx), plane], places[:-1])(*known)
        out_o = across(out_o)
        pair, in_o = call(solve_in, [framed_pair, plane], places)(*known, held)
        return (*known, pair), inside(in_o), out_o, beside

    known, z_in, z_out, beside = start(xo, xm, (one, two, three), None)
    p, q, xm, *sums, dots = call(
        inner_first, [block, block, middle_shape, *rows, (1, 128)], places + [VMEM] * 6, field
    )(*known, fx, fy, fz, fye, e, b)
    qo, xo, *sums, dots = call(outer_first, [ends_shape, ends_shape, *rows, (1, 128)], [VMEM] * 11)(
        p, q, *sums, z_in, z_out, fze, s, vectors, dots
    )
    known, z_in, z_out, _ = start(xo, xm, sums, beside)
    w, v, last_dots = call(inner_last, [block, block, (1, 128)], places + [VMEM] * 8, field)(
        *known, fx, fy, fz, fye, e, b, q, qo
    )
    vo, dots = call(outer_last, [ends_shape, (1, 128)], [VMEM] * 7)(w, v, z_in, z_out, fze, last_dots, dots)
    count = parts * layers
    gathered = lax.all_to_all(jnp.broadcast_to(dots, (count, 128)), ALL, 0, 0, tiled=True)
    return tuple(
        call(
            combine,
            [block, block],
            [VMEM] * 8,
            [pltpu.VMEM(block, F32)] * 2 + [pltpu.SemaphoreType.DMA((2, nz))],
            out_space=HBM,
        )(gathered, p, w, q, qo, v, vo, b)
    )


def solution(mesh):
    return jax.shard_map(
        local,
        mesh=mesh,
        in_specs=(P("gz", "gy", None), P(), P(None, "gz", "gy"), P(), P("gz", "gy", None)),
        out_specs=(P("gz", "gy", None), P("gz", "gy", None)),
        check_vma=False,
    )
```

```python
import math

import jax
import jax.numpy as jnp
import ml_dtypes
import numpy as np
from jax import lax
from jax.experimental import pallas as pl
from jax.experimental.pallas import tpu as pltpu
from jax.sharding import PartitionSpec as P

F32 = jnp.float32
SHIFT = 0.0016
VMEM = pl.BlockSpec(memory_space=pltpu.VMEM)
HBM = pl.BlockSpec(memory_space=pltpu.HBM)
ALL = ("gz", "gy")
STEP = 64


def line_tables(total, parts):
    rows = total // parts
    theta = math.acosh(1.0 + SHIFT / 2.0)
    near = np.cosh(theta * (np.arange(total) + 0.5))
    far = near[::-1]
    norm = math.sinh(theta) * math.sinh(total * theta)
    at = np.arange(total)
    green = np.where(at[:, None] <= at[None, :], near[:, None] * far[None, :], far[:, None] * near[None, :]) / norm
    blocks, vectors, scalars = [], [], np.zeros((parts, 8))
    for d in range(parts):
        own = slice(d * rows, (d + 1) * rows)
        low, high = math.cosh(theta * d * rows), math.cosh(theta * (d + 1) * rows)
        flow, fhigh = math.cosh(theta * (total - d * rows)), math.cosh(theta * (total - (d + 1) * rows))
        g = green[own, own].astype(np.float32)
        head = g.astype(ml_dtypes.bfloat16)
        tail = (g - head.astype(np.float32)).astype(ml_dtypes.bfloat16)
        blocks.append(np.concatenate([head, tail, head], axis=1))
        columns = [near[own] / high, far[own] / flow, low * far[own] / norm, fhigh * near[own] / norm]
        vectors.append(np.stack([np.broadcast_to(c[:, None], (rows, 128)) for c in columns]))
        for k in range(1, parts):
            other = d ^ k
            if other < d:
                scalars[d, k] = math.cosh(theta * (other + 1) * rows) / low
            else:
                scalars[d, 4 + k] = math.cosh(theta * (total - other * rows)) / fhigh
    return np.stack(blocks), np.stack(vectors).astype(np.float32), np.repeat(scalars[..., None], 128, 2).astype(np.float32)


def call(body, outs, ins, scratch=(), out_space=VMEM):
    return pl.pallas_call(
        body,
        out_shape=[s if hasattr(s, "dtype") else jax.ShapeDtypeStruct(s, F32) for s in outs],
        in_specs=ins,
        out_specs=[out_space] * len(outs),
        scratch_shapes=list(scratch),
        compiler_params=pltpu.CompilerParams(vmem_limit_bytes=24 * 2**20),
    )


def rows_at(start):
    return slice(start, start + STEP)


def sublane(shape):
    return lax.broadcasted_iota(jnp.int32, shape, 0)


def lane(shape):
    return lax.broadcasted_iota(jnp.int32, shape, 1)


def recip(x):
    r = pl.reciprocal(x, approx=True)
    return r * (2.0 - x * r)


def fold(x):
    return sum(x[r : r + 8] for r in range(0, x.shape[0], 8))


def folded(x):
    x = fold(x)
    return sum(x[:, c : c + 128] for c in range(0, x.shape[1], 128))


def lookup(labels, table):
    low = jnp.where(labels == 1, table[1], table[0])
    high = jnp.where(labels == 3, table[3], table[2])
    return jnp.where(labels >= 2, high, low)


def wide(column, width):
    return jnp.concatenate([column] * (width // 128), axis=1)


def ends(value, low, high):
    return jnp.concatenate([value[:, :128] + low, value[:, 128:-128], value[:, -128:] + high], axis=1)


def local(labels, phase_table, collector_mask, collector_value, source):
    nz, ny, nx = labels.shape
    parts = lax.axis_size("gy")
    layers = lax.axis_size("gz")
    block = (nz, ny, nx)
    plane = (1, ny, nx)
    edge = (nz, 8, nx)
    framed = (nz, ny + 16, nx)
    starts = range(0, ny, STEP)
    outer = sorted({0, nz - 1})
    middle = [z for z in range(nz) if z not in outer]
    ends_shape, middle_shape = (len(outer), ny, nx), (len(middle), ny, nx)
    green, vectors, scalars = line_tables(ny * parts, parts)
    green, vectors, scalars = jnp.asarray(green), jnp.asarray(vectors), jnp.asarray(scalars)

    def pick(z, first, second):
        return first.at[outer.index(z)] if z in outer else second.at[middle.index(z)]

    def swap(value, axis, size, partner):
        return lax.ppermute(value, axis, [(i, partner(i) % size) for i in range(size)])

    def inside(value):
        return swap(value, "gz", layers, lambda i: i ^ 1)

    def across(value):
        def partner(i, j):
            k = i + 1 if i % 2 else i - 1
            return (k, j) if 0 <= k < layers else (i, j ^ 1)
        pairs = [(i, j, *partner(i, j)) for i in range(layers) for j in range(parts)]
        return lax.ppermute(value, ALL, [(i * parts + j, k * parts + m) for i, j, k, m in pairs])

    def crosswise(value, step):
        return swap(value, "gy", parts, lambda i: i ^ step)

    def even(axis):
        return lax.axis_index(axis) % 2 == 0

    def side(inner):
        return jnp.where(even("gz") == inner, jnp.int32(nz - 1), jnp.int32(0))

    def border(labels, out_o, sem):
        copy = pltpu.make_async_copy(labels.at[pl.ds(side(False), 1)], out_o, sem)
        copy.start()
        copy.wait()

    def borders(labels, in_o, one_o, three_o, first, last, sems):
        copies = [
            pltpu.make_async_copy(labels.at[pl.ds(side(True), 1)], in_o, sems.at[0]),
            pltpu.make_async_copy(labels.at[:, pl.ds(0, 8)], first, sems.at[1]),
            pltpu.make_async_copy(labels.at[:, pl.ds(ny - 8, 8)], last, sems.at[2]),
        ]
        for copy in copies:
            copy.start()
        for copy in copies:
            copy.wait()
        for z in range(nz):
            low, high = first[z, 0:1, :], last[z, 7:8, :]
            one_o[z : z + 1, :] = jnp.where(even("gy"), high, low)
            three_o[z : z + 1, :] = jnp.where(even("gy"), low, high)

    sent = [jax.ShapeDtypeStruct(shape, jnp.int32) for shape in (plane, (nz, nx), (nz, nx))]
    out_o = call(border, sent[:1], [HBM], [pltpu.SemaphoreType.DMA])(labels)[0]
    in_o, one, three = call(
        borders, sent, [HBM], [pltpu.VMEM(edge, jnp.int32)] * 2 + [pltpu.SemaphoreType.DMA((3,))]
    )(labels)
    out_o, in_o = across(out_o), inside(in_o)
    one, three = crosswise(one, 1), crosswise(three, 3)

    head = jnp.concatenate([phase_table, collector_value])
    packed = jnp.concatenate(
        [jnp.pad(head, (0, ny - head.shape[0]))[None], collector_mask.reshape(2 * nz, ny).astype(F32)]
    )

    def halves(settings):
        return [wide(settings[n : n + 1, :], nx) for n in range(4)]

    def faces(labels, packed, source, k_o, fx_o, fy_o, fz_o, d_o, e_o, b_o, settings, held, framed_k, sem):
        copy = pltpu.make_async_copy(source, held, sem)
        copy.start()
        for n in range(6):
            value = jnp.broadcast_to(packed[0:1, n : n + 1], (1, 128))
            settings[n : n + 1, :] = 0.5 / value if n < 4 else value
        columns = jnp.transpose(packed[1 : 2 * nz + 1, :])
        table = halves(settings)
        values = [settings[4 + n : 5 + n, :] for n in range(2)]
        for z in range(nz):
            for r in starts:
                k = lookup(labels[z, rows_at(r), :], table)
                k_o[z, rows_at(r), :] = k
                framed_k[z, rows_at(r + 8), :] = k
            framed_k[z, ny + 8 : ny + 16, :] = framed_k[z, ny : ny + 8, :]
            fy_o[z, 0:8, :] = jnp.zeros((8, nx), F32)
        copy.wait()
        sub, across, side = sublane((STEP, nx)), lane((STEP, nx)), lane((STEP, 128))
        for z in range(nz):
            for r in starts:
                at = rows_at(r)
                k = k_o[z, at, :]
                fy = recip(k + framed_k[z, rows_at(r + 9), :])
                if r + STEP == ny:
                    fy = jnp.where(sub == STEP - 1, 0.0, fy)
                fy_o[z, rows_at(r + 8), :] = fy
                fx = jnp.where(across == nx - 1, 0.0, recip(k + pltpu.roll(k, nx - 1, 1)))
                d = fy + fy_o[z, rows_at(r + 7), :] + (fx + pltpu.roll(fx, 1, 1))
                if z > 0:
                    d = d + fz_o[z - 1, at, :]
                if z < nz - 1:
                    fz = recip(k + k_o[z + 1, at, :])
                    fz_o[z, at, :] = fz
                    d = d + fz
                low = jnp.where(side == 0, recip(k[:, :128]) * columns[at, z : z + 1], 0.0)
                high = jnp.where(side == 127, recip(k[:, -128:]) * columns[at, nz + z : nz + z + 1], 0.0)
                e_o[z, at, :] = jnp.concatenate([low, high], axis=1)
                d_o[z, at, :] = ends(d, low, high)
                b_o[z, at, :] = ends(held[z, at, :], low * values[0], high * values[1])
                fx_o[z, at, :] = fx

    k, fx, fy, fz, d, e, b, settings = call(
        faces,
        [block, block, (nz, ny + 8, nx), (nz - 1, ny, nx), block, (nz, ny, 256), block, (8, 128)],
        [VMEM, VMEM, HBM],
        [pltpu.VMEM(block, F32), pltpu.VMEM(framed, F32), pltpu.SemaphoreType.DMA],
    )(labels, packed, source)

    def weighted(x, my, vectors, r, carry):
        return (
            carry[0] + fold(x * wide(vectors[my, 0, rows_at(r), :], nx)),
            carry[1] + fold(x * wide(vectors[my, 1, rows_at(r), :], nx)),
        )

    def sums_out(my, sums, z, outs):
        right, left = (jnp.sum(v, 0, keepdims=True) for v in sums)
        for step, out in enumerate(outs, 1):
            out[z : z + 1, :] = jnp.where((my ^ step) > my, right, left)

    zero = lambda: jnp.zeros((8, nx), F32)
    none = lambda: jnp.zeros((8, 128), F32)

    def scaled(settings, k, y_one, y_three, z_in, z_out, d, b, vectors, s_o, xo_o, xm_o, fye_o, fze_o, one, two, three):
        my, level = lax.axis_index("gy"), lax.axis_index("gz")
        has_low, has_high = (my > 0).astype(F32), (my < parts - 1).astype(F32)
        has_below, has_above = (level > 0).astype(F32), (level < layers - 1).astype(F32)
        sub = sublane((STEP, nx))
        table = halves(settings)
        for z in range(nz):
            ones, threes = y_one[z : z + 1, :], y_three[z : z + 1, :]
            ylo, yhi = jnp.where(even("gy"), threes, ones), jnp.where(even("gy"), ones, threes)
            first = has_low * recip(lookup(ylo, table) + k[z, 0:1, :])
            last = has_high * recip(lookup(yhi, table) + k[z, ny - 1 : ny, :])
            fye_o[z, 0:1, :] = first
            fye_o[z, 1:2, :] = last
            carry = (zero(), zero())
            for r in starts:
                at = rows_at(r)
                diagonal = d[z, at, :]
                if r == 0:
                    diagonal = diagonal + jnp.where(sub == 0, first, 0.0)
                if r + STEP == ny:
                    diagonal = diagonal + jnp.where(sub == STEP - 1, last, 0.0)
                if z == 0:
                    face = has_below * recip(lookup(jnp.where(even("gz"), z_out[0, at, :], z_in[0, at, :]), table) + k[z, at, :])
                    fze_o[0, at, :] = face
                    diagonal = diagonal + face
                if z == nz - 1:
                    face = has_above * recip(lookup(jnp.where(even("gz"), z_in[0, at, :], z_out[0, at, :]), table) + k[z, at, :])
                    fze_o[1, at, :] = face
                    diagonal = diagonal + face
                s = lax.rsqrt(diagonal)
                x = s * b[z, at, :]
                s_o[z, at, :] = s
                pick(z, xo_o, xm_o)[at, :] = x
                carry = weighted(x, my, vectors, r, carry)
            sums_out(my, carry, z, (one, two, three))
            low, high = s_o[z, 0:1, :], s_o[z, ny - 1 : ny, :]
            one[nz + z : nz + z + 1, :] = jnp.where(even("gy"), high, low)
            three[nz + z : nz + z + 1, :] = jnp.where(even("gy"), low, high)

    s, xo, xm, fye, fze, one, two, three = call(
        scaled,
        [block, ends_shape, middle_shape, edge, (2, ny, nx), (2 * nz, nx), (nz, nx), (2 * nz, nx)],
        [VMEM] * 9,
    )(settings, k, one, three, in_o, out_o, d, b, vectors)

    def lines(xo, xm, green, out):
        my = lax.axis_index("gy")
        for z in range(nz):
            x = pick(z, xo, xm)[...]
            head = x.astype(jnp.bfloat16)
            tail = (x - head.astype(F32)).astype(jnp.bfloat16)
            stack = jnp.concatenate([head, head, tail], axis=0)
            out[z] = jnp.dot(green[my], stack, preferred_element_type=F32)

    def solve(z, x, part, s, vectors, scalars, one, two, three, s_one, s_three, put):
        my = lax.axis_index("gy")
        got = [r[pl.ds(z, 1), :] for r in (one, two, three)]
        left = sum(wide(scalars[my, n + 1 : n + 2, :], nx) * got[n] for n in range(3))
        right = sum(wide(scalars[my, n + 5 : n + 6, :], nx) * got[n] for n in range(3))
        ones, threes = s_one[pl.ds(nz + z, 1), :], s_three[pl.ds(nz + z, 1), :]
        for r in starts:
            at = rows_at(r)
            g = part[z, at, :] + (wide(vectors[my, 2, at, :], nx) * left + wide(vectors[my, 3, at, :], nx) * right)
            put(r + 8, s[z, at, :] * g)
            if r == 0:
                beside = (2.0 + SHIFT) * g[0:1] - g[1:2] - x[0:1, :]
                put(7, jnp.where(even("gy"), threes, ones) * beside)
            if r + STEP == ny:
                beside = (2.0 + SHIFT) * g[-1:] - g[-2:-1] - x[ny - 1 : ny, :]
                put(ny + 8, jnp.where(even("gy"), ones, threes) * beside)

    def solve_out(part, s, xo, xm, vectors, scalars, one, two, three, s_one, s_three, held_o, out_o):
        def put(r, value):
            held_o[r : r + value.shape[0], :] = value
            if value.shape[0] == STEP:
                out_o[0, rows_at(r - 8), :] = value
        z = side(False)
        place = xo.at[jnp.where(z == 0, 0, 1)]
        solve(z, place, part, s, vectors, scalars, one, two, three, s_one, s_three, put)

    def solve_in(part, s, xo, xm, vectors, scalars, one, two, three, s_one, s_three, held, p_o, in_o):
        z = side(True)
        n = jnp.where(z == 0, 0, 1)

        def put(r, value):
            p_o[n, r : r + value.shape[0], :] = value
            if value.shape[0] == STEP:
                in_o[0, rows_at(r - 8), :] = value
        solve(z, xo.at[n], part, s, vectors, scalars, one, two, three, s_one, s_three, put)
        for r in range(0, ny + 16, 16):
            p_o[1 - n, r : r + 16, :] = held[r : r + 16, :]

    def total(value):
        return jnp.sum(jnp.sum(value, 0, keepdims=True), 1, keepdims=True)

    def dots_out(out, sums, first):
        at = lane((1, 128))
        row = jnp.zeros((1, 128), F32)
        for n, value in enumerate(sums, first):
            row = jnp.where(at == n, total(value), row)
        out[...] = row

    def operator(read, z, r, fx, fy, fz, fye, e):
        at = rows_at(r)
        v = read(z, r + 8)
        q = fy[z, rows_at(r + 8), :] * (v - read(z, r + 9)) + fy[z, rows_at(r + 7), :] * (v - read(z, r + 7))
        sub = sublane((STEP, nx))
        if r == 0:
            q = q + jnp.where(sub == 0, fye[z, 0:1, :], 0.0) * (v - read(z, r + 7))
        if r + STEP == ny:
            q = q + jnp.where(sub == STEP - 1, fye[z, 1:2, :], 0.0) * (v - read(z, r + 9))
        flow = fx[z, at, :] * (v - pltpu.roll(v, nx - 1, 1))
        q = q + (flow - pltpu.roll(flow, 1, 1))
        if z > 0:
            q = q + fz[z - 1, at, :] * (v - read(z - 1, r + 8))
        if z < nz - 1:
            q = q + fz[z, at, :] * (v - read(z + 1, r + 8))
        edges = e[z, at, :]
        return v, ends(q, edges[:, :128] * v[:, :128], edges[:, 128:] * v[:, -128:])

    def fill(part, s, xo, xm, vectors, scalars, one, two, three, s_one, s_three, p_outer, p_o, field):
        for z in middle:
            def put(r, value):
                field[z, r : r + value.shape[0], :] = value
                if value.shape[0] == STEP:
                    p_o[z, rows_at(r - 8), :] = value
            solve(z, pick(z, xo, xm), part, s, vectors, scalars, one, two, three, s_one, s_three, put)
        for n, z in enumerate(outer):
            for r in starts:
                p_o[z, rows_at(r), :] = p_outer[n, rows_at(r + 8), :]

        def read(z, r):
            return p_outer[outer.index(z), rows_at(r), :] if z in outer else field[z, rows_at(r), :]
        return read

    def inner_first(part, s, xo, xm, vectors, scalars, one, two, three, s_one, s_three, p_outer, fx, fy, fz, fye, e, b,
                    p_o, q_o, xm_o, one_o, two_o, three_o, dots, field):
        my = lax.axis_index("gy")
        read = fill(part, s, xo, xm, vectors, scalars, one, two, three, s_one, s_three, p_outer, p_o, field)
        bp, pq = none(), none()
        for z in outer + middle:
            carry = (zero(), zero())
            for r in starts:
                at = rows_at(r)
                v, image = operator(read, z, r, fx, fy, fz, fye, e)
                bp = bp + folded(b[z, at, :] * v)
                q_o[z, at, :] = image
                if z in middle:
                    scaled_image = s[z, at, :] * image
                    xm_o[middle.index(z), at, :] = scaled_image
                    carry = weighted(scaled_image, my, vectors, r, carry)
                    pq = pq + folded(v * image)
            if z in middle:
                sums_out(my, carry, z, (one_o, two_o, three_o))
        dots_out(dots, (bp, pq), 0)

    def image_of(z, ends, whole, at):
        return ends[outer.index(z), at, :] if z in outer else whole[z, at, :]

    def outside(z, r, v, image, z_in, z_out, fze):
        at = rows_at(r)
        if z == 0:
            image = image + fze[0, at, :] * (v - jnp.where(even("gz"), z_out[0, at, :], z_in[0, at, :]))
        if z == nz - 1:
            image = image + fze[1, at, :] * (v - jnp.where(even("gz"), z_in[0, at, :], z_out[0, at, :]))
        return image

    def outer_first(p, q, one, two, three, z_in, z_out, fze, s, vectors, dots, qo_o, xo_o, one_o, two_o, three_o, dots_o):
        my = lax.axis_index("gy")
        pq = none()
        for z in outer:
            carry = (zero(), zero())
            for r in starts:
                at = rows_at(r)
                v = p[z, at, :]
                image = outside(z, r, v, q[z, at, :], z_in, z_out, fze)
                scaled_image = s[z, at, :] * image
                qo_o[outer.index(z), at, :] = image
                xo_o[outer.index(z), at, :] = scaled_image
                carry = weighted(scaled_image, my, vectors, r, carry)
                pq = pq + folded(v * image)
            sums_out(my, carry, z, (one_o, two_o, three_o))
        for z in middle:
            for got, out in ((one, one_o), (two, two_o), (three, three_o)):
                out[z : z + 1, :] = got[z : z + 1, :]
        dots_out(dots_o, (none(), pq), 0)
        dots_o[...] = dots_o[...] + dots[...]

    def inner_last(part, s, xo, xm, vectors, scalars, one, two, three, s_one, s_three, p_outer, fx, fy, fz, fye, e, b, q, qo,
                   w_o, v_o, dots, field):
        read = fill(part, s, xo, xm, vectors, scalars, one, two, three, s_one, s_three, p_outer, w_o, field)
        bw, qw, wv = none(), none(), none()
        for z in range(nz):
            for r in starts:
                at = rows_at(r)
                w, image = operator(read, z, r, fx, fy, fz, fye, e)
                bw = bw + folded(b[z, at, :] * w)
                qw = qw + folded(image_of(z, qo, q, at) * w)
                wv = wv + folded(image * w)
                v_o[z, at, :] = image
        dots_out(dots, (bw, qw, wv), 2)

    def outer_last(w, v, z_in, z_out, fze, dots_first, dots, v_o, dots_o):
        wv = none()
        for n, z in enumerate(outer):
            for r in starts:
                at = rows_at(r)
                field, image = w[z, at, :], v[z, at, :]
                full = outside(z, r, field, image, z_in, z_out, fze)
                v_o[n, at, :] = full
                wv = wv + folded((full - image) * field)
        dots_out(dots_o, (wv,), 4)
        dots_o[...] = dots_o[...] + (dots[...] + dots_first[...])

    def combine(gathered, p, w, q, qo, v, vo, b, x_o, r_o, x_held, r_held, sems):
        sums = jnp.sum(gathered[...], 0, keepdims=True)
        at = lane((1, 128))
        bp, pq, bw, qw, wv = (jnp.sum(jnp.where(at == n, sums, 0.0), 1, keepdims=True) for n in range(5))
        step = bp / pq
        product = bp - step * (bw + pq) + step * step * qw
        more = 1.0 + product / bp
        curvature = more * more * pq - 2.0 * more * step * qw + step * step * wv
        second = product / curvature
        along = jnp.broadcast_to(step + second * more, (STEP, nx))
        across = jnp.broadcast_to(second * step, (STEP, nx))
        copies = []
        for z in range(nz):
            for r in starts:
                at = rows_at(r)
                x_held[z, at, :] = along * p[z, at, :] - across * w[z, at, :]
                r_held[z, at, :] = b[z, at, :] - along * image_of(z, qo, q, at) + across * image_of(z, vo, v, at)
                for n, (held, out) in enumerate(((x_held, x_o), (r_held, r_o))):
                    some = pl.ds(r, STEP)
                    copies.append(pltpu.make_async_copy(held.at[z, some], out.at[z, some], sems.at[n, z, r // STEP]))
                    copies[-1].start()
        for copy in copies:
            copy.wait()

    def pass_on(one, three, one_o, three_o):
        one_o[...] = one[...]
        three_o[...] = three[...]

    def gather(sums):
        one, two, three = sums
        two = crosswise(two, 2)
        one, three = call(pass_on, [one.shape, three.shape], [VMEM] * 2)(one, three)
        return [crosswise(one, 1), two, crosswise(three, 3)]

    field = [pltpu.VMEM(framed, F32)]
    rows = [(nz, nx)] * 3
    framed_pair = (len(outer), ny + 16, nx)

    places = [VMEM] * 12

    def start(xo, xm, sums, beside):
        got = gather(sums)
        beside = beside or (got[0], got[2])
        part = call(lines, [block], [VMEM] * 3)(xo, xm, green)[0]
        known = (part, s, xo, xm, vectors, scalars, *got, *beside)
        held, out_o = call(solve_out, [(ny + 16, nx), plane], places[:-1])(*known)
        out_o = across(out_o)
        pair, in_o = call(solve_in, [framed_pair, plane], places)(*known, held)
        return (*known, pair), inside(in_o), out_o, beside

    known, z_in, z_out, beside = start(xo, xm, (one, two, three), None)
    p, q, xm, *sums, dots = call(
        inner_first, [block, block, middle_shape, *rows, (1, 128)], places + [VMEM] * 6, field
    )(*known, fx, fy, fz, fye, e, b)
    qo, xo, *sums, dots = call(outer_first, [ends_shape, ends_shape, *rows, (1, 128)], [VMEM] * 11)(
        p, q, *sums, z_in, z_out, fze, s, vectors, dots
    )
    known, z_in, z_out, _ = start(xo, xm, sums, beside)
    w, v, last_dots = call(inner_last, [block, block, (1, 128)], places + [VMEM] * 8, field)(
        *known, fx, fy, fz, fye, e, b, q, qo
    )
    vo, dots = call(outer_last, [ends_shape, (1, 128)], [VMEM] * 7)(w, v, z_in, z_out, fze, last_dots, dots)
    count = parts * layers
    gathered = lax.all_to_all(jnp.broadcast_to(dots, (count, 128)), ALL, 0, 0, tiled=True)
    return tuple(
        call(
            combine,
            [block, block],
            [VMEM] * 8,
            [pltpu.VMEM(block, F32)] * 2 + [pltpu.SemaphoreType.DMA((2, nz, len(starts)))],
            out_space=HBM,
        )(gathered, p, w, q, qo, v, vo, b)
    )


def solution(mesh):
    return jax.shard_map(
        local,
        mesh=mesh,
        in_specs=(P("gz", "gy", None), P(), P(None, "gz", "gy"), P(), P("gz", "gy", None)),
        out_specs=(P("gz", "gy", None), P("gz", "gy", None)),
        check_vma=False,
    )
```
